32 devices in a mesh: rows: 4 (over z), cols: 2 (over x), rep: 4 (over y, core).
Axes of the slice: x: 2, y: 2, z: 4, core: 2. Of those that a mesh axis runs over, the one named last changes fastest.
Arguments:
- feature_map: bfloat16 [4, 32, 32, 384], P('rep', 'rows', 'cols'), may hold values from -6 to 6
- dw_kernel: float32 [7, 7, 384], replicated, may hold values from -0.875 to 0.875
- dw_bias: float32 [384], replicated, may hold values from -3 to 3
- layer_norm_gain: float32 [384], replicated, may hold values from 0.5 to 1.5
- layer_norm_bias: float32 [384], replicated, may hold values from -3 to 3
- w_expand: bfloat16 [384, 1536], replicated, may hold values from -0.3125 to 0.3125
- b_expand: float32 [1536], replicated, may hold values from -3 to 3
- w_reduce: bfloat16 [1536, 384], replicated, may hold values from -0.15625 to 0.15625
- b_reduce: float32 [384], replicated, may hold values from -3 to 3
- layer_scale: float32 [384], replicated, may hold values from 0.5 to 1.5
- cotangent: bfloat16 [4, 32, 32, 384], P('rep', 'rows', 'cols'), may hold values from -6 to 6
Outputs:
- block_out: bfloat16 [4, 32, 32, 384], P('rep', 'rows', 'cols')
- grad_input: bfloat16 [4, 32, 32, 384], P('rep', 'rows', 'cols')
- grad_expand: float32 [384, 1536], P('rep', ('rows', 'cols'))
- grad_reduce_t: float32 [384, 1536], P('rep', ('rows', 'cols'))
- grad_kernel: float32 [7, 7, 384], replicated
- grad_vectors: float32 [5, 384], replicated
- grad_bexp: float32 [1536], replicated
The draws below stay inside these ranges and needn't reach their ends.
All inputs are finite; a program needn't handle non-finite values.
Results may differ from the reference program's by a relative error of at most 0.0062.
Values may be sent and summed in bfloat16 or wider, within the bound.
A program may use at most 64 MiB of HBM per device.

```python
import jax
import jax.numpy as jnp
from jax import lax

D = 384
FF = 1536
REGIONS = 4
H = 32
W = 32
PIXELS = 4096


def level_of(own_key, dims, split, smallest, top_value):
    def one(position, parts):
        heights = jax.random.uniform(jax.random.fold_in(jax.random.fold_in(own_key, 6), position), (parts,), jnp.float32, smallest / len(split), top_value / len(split))
        return jnp.repeat(jnp.exp(heights), dims[position] // parts).reshape((-1,) + (1,) * (len(dims) - position - 1))

    gain = one(*split[0])
    for cut in split[1:]:
        gain = gain * one(*cut)
    return gain


def gaussian(own_key, shape, scale, most, shards=(), held_as=jnp.bfloat16):
    level = level_of(own_key, shape, shards, -0.22, 0.18) if shards else 1.0
    array = jax.random.normal(own_key, shape, jnp.float32) * scale * level
    return jnp.minimum(jnp.maximum(array, -most), most).astype(held_as)


def setup_inputs(seed: int = 0) -> dict:
    streams_of = jax.random.split(jax.random.key(seed), 12)
    feature_map = gaussian(streams_of[0], (REGIONS, H, W, D), 1.0, 6.0, ((0, 4), (1, 4), (2, 2)))
    dw_kernel = gaussian(streams_of[1], (7, 7, D), 49 ** -0.5, 0.875, (), jnp.float32)
    dw_bias = gaussian(streams_of[2], (D,), 0.5, 3.0, (), jnp.float32)
    layer_norm_gain = jnp.clip(jax.random.uniform(streams_of[3], (D,), jnp.float32, 0.5, 1.5), 0.5, 1.5)
    layer_norm_bias = gaussian(streams_of[4], (D,), 0.5, 3.0, (), jnp.float32)
    w_expand = gaussian(streams_of[5], (D, FF), D ** -0.5, 0.3125)
    b_expand = gaussian(streams_of[6], (FF,), 0.5, 3.0, (), jnp.float32)
    w_reduce = gaussian(streams_of[7], (FF, D), FF ** -0.5, 0.15625)
    b_reduce = gaussian(streams_of[8], (D,), 0.5, 3.0, (), jnp.float32)
    layer_scale = jnp.clip(jax.random.uniform(streams_of[9], (D,), jnp.float32, 0.5, 1.5), 0.5, 1.5)
    cotangent = gaussian(streams_of[10], (REGIONS, H, W, D), 1.0, 6.0, ((0, 4), (1, 4), (2, 2)))
    return {"feature_map": feature_map, "dw_kernel": dw_kernel, "dw_bias": dw_bias, "layer_norm_gain": layer_norm_gain, "layer_norm_bias": layer_norm_bias, "w_expand": w_expand, "b_expand": b_expand, "w_reduce": w_reduce, "b_reduce": b_reduce, "layer_scale": layer_scale, "cotangent": cotangent}


EPS = 1e-06
INV_ROOT_TWO = 0.7071067811865476
INV_ROOT_TWO_PI = 0.3989422804014327

def depthwise(padded, kernel, height, width):
    total = jnp.zeros((height, width, padded.shape[-1]), jnp.float32)
    for i in range(7):
        for j in range(7):
            total = total + kernel[i, j] * padded[i:i + height, j:j + width].astype(jnp.float32)
    return total

def front_pass(xpad, gout, dw_kernel, dw_bias, layer_norm_gain, layer_norm_bias, w_expand, b_expand, w_reduce, b_reduce, layer_scale, height, width):
    chans = xpad.shape[-1]
    conv = depthwise(xpad, dw_kernel, height, width) + dw_bias
    flat = conv.reshape(-1, chans)
    centered_input = flat - lax.optimization_barrier(jnp.mean(flat, axis=-1, keepdims=True))
    inverse_deviation = lax.rsqrt(lax.optimization_barrier(jnp.mean(centered_input * centered_input, axis=-1, keepdims=True)) + EPS)
    standardized_input = centered_input * inverse_deviation
    normalized_rows = (standardized_input * layer_norm_gain + layer_norm_bias).astype(jnp.bfloat16)
    pre = jnp.dot(normalized_rows, w_expand, preferred_element_type=jnp.float32) + b_expand
    cdf = 0.5 * (1.0 + lax.erf(pre * INV_ROOT_TWO))
    act = (pre * cdf).astype(jnp.bfloat16)
    branch = jnp.dot(act, w_reduce, preferred_element_type=jnp.float32) + b_reduce
    inner = xpad[3:3 + height, 3:3 + width].reshape(-1, chans).astype(jnp.float32)
    block_out = (inner + layer_scale * branch).astype(jnp.bfloat16).reshape(height, width, chans)
    grad = gout.reshape(-1, chans).astype(jnp.float32)
    scaled = grad * layer_scale
    g_branch = scaled.astype(jnp.bfloat16)
    g_scale = lax.optimization_barrier(jnp.sum(grad * branch, axis=0))
    g_breduce = lax.optimization_barrier(jnp.sum(scaled, axis=0))
    grad_reduce_t = lax.dot_general(g_branch, act, (((0,), (0,)), ((), ())), preferred_element_type=jnp.float32)
    g_act = lax.dot_general(g_branch, w_reduce, (((1,), (1,)), ((), ())), preferred_element_type=jnp.float32)
    pdf = jnp.exp(-0.5 * pre * pre) * INV_ROOT_TWO_PI
    g_pre = g_act * (cdf + pre * pdf)
    g_bexp = lax.optimization_barrier(jnp.sum(g_pre, axis=0))
    g_pre_b = g_pre.astype(jnp.bfloat16)
    grad_expand = lax.dot_general(normalized_rows, g_pre_b, (((0,), (0,)), ((), ())), preferred_element_type=jnp.float32)
    grad_normalized = lax.dot_general(g_pre_b, w_expand, (((1,), (1,)), ((), ())), preferred_element_type=jnp.float32)
    grad_norm_gain = lax.optimization_barrier(jnp.sum(grad_normalized * standardized_input, axis=0))
    g_lnbias = lax.optimization_barrier(jnp.sum(grad_normalized, axis=0))
    scaled_grad_input = grad_normalized * layer_norm_gain
    grad_convolution = inverse_deviation * (scaled_grad_input - lax.optimization_barrier(jnp.mean(scaled_grad_input, axis=-1, keepdims=True)) - standardized_input * lax.optimization_barrier(jnp.mean(scaled_grad_input * standardized_input, axis=-1, keepdims=True)))
    g_dwbias = lax.optimization_barrier(jnp.sum(grad_convolution, axis=0))
    vectors = jnp.stack([g_dwbias, grad_norm_gain, g_lnbias, g_breduce, g_scale])
    return (block_out, grad_convolution.reshape(height, width, chans), grad_expand, grad_reduce_t, vectors, g_bexp)

def back_pass(gpad, xpad, gout, dw_kernel, height, width):
    inner = gpad[3:3 + height, 3:3 + width]
    grad_in = gout.astype(jnp.float32)
    kernel_rows = []
    for i in range(7):
        row_terms = []
        for j in range(7):
            part = xpad[i:i + height, j:j + width].astype(jnp.float32)
            row_terms.append(lax.optimization_barrier(jnp.sum(inner * part, axis=(0, 1))))
            grad_in = grad_in + dw_kernel[i, j] * gpad[6 - i:6 - i + height, 6 - j:6 - j + width]
        kernel_rows.append(jnp.stack(row_terms))
    return (grad_in.astype(jnp.bfloat16), jnp.stack(kernel_rows))

def reference(feature_map, dw_kernel, dw_bias, layer_norm_gain, layer_norm_bias, w_expand, b_expand, w_reduce, b_reduce, layer_scale, cotangent):
    height, width = (feature_map.shape[1], feature_map.shape[2])

    def region(pair):
        xr, gr = pair
        xpad = jnp.pad(xr, ((3, 3), (3, 3), (0, 0)))
        block_out, grad_convolution, gexp, gred, vectors, gbexp = front_pass(xpad, gr, dw_kernel, dw_bias, layer_norm_gain, layer_norm_bias, w_expand, b_expand, w_reduce, b_reduce, layer_scale, height, width)
        gpad = jnp.pad(grad_convolution, ((3, 3), (3, 3), (0, 0)))
        grad_in, gker = back_pass(gpad, xpad, gr, dw_kernel, height, width)
        return (block_out, grad_in, gexp, gred, gker, vectors, gbexp)
    outs = lax.map(region, (feature_map, cotangent))
    scale = 1.0 / jnp.sqrt(jnp.float32(PIXELS))
    return (outs[0], outs[1], lax.optimization_barrier(jnp.sum(outs[2], axis=0)) * scale, lax.optimization_barrier(jnp.sum(outs[3], axis=0)) * scale, lax.optimization_barrier(jnp.sum(outs[4], axis=0)) * scale, lax.optimization_barrier(jnp.sum(outs[5], axis=0)) * scale, lax.optimization_barrier(jnp.sum(outs[6], axis=0)) * scale)
```

```python
import functools

import jax
import jax.numpy as jnp
from jax import lax
from jax.experimental import pallas as pl
from jax.experimental.pallas import tpu as pltpu
from jax.sharding import PartitionSpec as P

MESH = pl.DeviceIdType.MESH
F32, BF16 = jnp.float32, jnp.bfloat16
LANES = 128
PIECE = 16
ORDERS = ("yxz", "xyz", "zyx", "xyz", "yxz", "xyz")
DIRECTIONS = ((-1, 0), (1, 0), (0, -1), (0, 1), (-1, -1), (-1, 1), (1, -1), (1, 1))
SIZES = {"y": 2, "x": 2, "z": 4}

EPS = 1e-06
INV_ROOT_TWO = 0.7071067811865476
INV_ROOT_TWO_PI = 0.3989422804014327


def extended(cells, sides, width):
    for axis, dim in sides:
        count = lax.axis_size(axis)
        ends = count - 1
        head = lax.slice_in_dim(cells, 0, width, axis=dim)
        tail = lax.slice_in_dim(cells, cells.shape[dim] - width, cells.shape[dim], axis=dim)
        cells = jnp.concatenate(
            [
                lax.ppermute(tail, axis, [(i, (i + 1) % count) for i in range(ends)]),
                cells,
                lax.ppermute(head, axis, [((i + 1) % count, i) for i in range(ends)]),
            ],
            axis=dim,
        )
    return cells


def depthwise(padded, kernel, height, width):
    total = jnp.zeros((height, width, padded.shape[-1]), jnp.float32)
    for i in range(7):
        for j in range(7):
            total = total + kernel[i, j] * padded[i : i + height, j : j + width].astype(jnp.float32)
    return total


def front_pass(
    xpad,
    gout,
    dw_kernel,
    dw_bias,
    layer_norm_gain,
    layer_norm_bias,
    w_expand,
    b_expand,
    w_reduce,
    b_reduce,
    layer_scale,
    height,
    width,
):
    chans = xpad.shape[-1]
    conv = depthwise(xpad, dw_kernel, height, width) + dw_bias
    flat = conv.reshape(-1, chans)
    centered_input = flat - jnp.mean(flat, axis=-1, keepdims=True)
    inverse_deviation = lax.rsqrt(
        jnp.mean(centered_input * centered_input, axis=-1, keepdims=True) + EPS
    )
    standardized_input = centered_input * inverse_deviation
    normalized_rows = (standardized_input * layer_norm_gain + layer_norm_bias).astype(jnp.bfloat16)
    pre = jnp.dot(normalized_rows, w_expand, preferred_element_type=jnp.float32) + b_expand
    cdf = 0.5 * (1.0 + lax.erf(pre * INV_ROOT_TWO))
    act = (pre * cdf).astype(jnp.bfloat16)
    branch = jnp.dot(act, w_reduce, preferred_element_type=jnp.float32) + b_reduce
    inner = xpad[3 : 3 + height, 3 : 3 + width].reshape(-1, chans).astype(jnp.float32)
    block_out = (inner + layer_scale * branch).astype(jnp.bfloat16).reshape(height, width, chans)
    grad = gout.reshape(-1, chans).astype(jnp.float32)
    scaled = grad * layer_scale
    g_branch = scaled.astype(jnp.bfloat16)
    g_scale = jnp.sum(grad * branch, axis=0)
    g_breduce = jnp.sum(scaled, axis=0)
    grad_reduce_t = lax.dot_general(
        g_branch, act, (((0,), (0,)), ((), ())), preferred_element_type=jnp.float32
    )
    g_act = lax.dot_general(
        g_branch, w_reduce, (((1,), (1,)), ((), ())), preferred_element_type=jnp.float32
    )
    pdf = jnp.exp(-0.5 * pre * pre) * INV_ROOT_TWO_PI
    g_pre = g_act * (cdf + pre * pdf)
    g_bexp = jnp.sum(g_pre, axis=0)
    g_pre_b = g_pre.astype(jnp.bfloat16)
    grad_expand = lax.dot_general(
        normalized_rows, g_pre_b, (((0,), (0,)), ((), ())), preferred_element_type=jnp.float32
    )
    grad_normalized = lax.dot_general(
        g_pre_b, w_expand, (((1,), (1,)), ((), ())), preferred_element_type=jnp.float32
    )
    grad_norm_gain = jnp.sum(grad_normalized * standardized_input, axis=0)
    g_lnbias = jnp.sum(grad_normalized, axis=0)
    scaled_grad_input = grad_normalized * layer_norm_gain
    grad_convolution = inverse_deviation * (
        scaled_grad_input
        - jnp.mean(scaled_grad_input, axis=-1, keepdims=True)
        - standardized_input
        * jnp.mean(scaled_grad_input * standardized_input, axis=-1, keepdims=True)
    )
    g_dwbias = jnp.sum(grad_convolution, axis=0)
    vectors = jnp.stack([g_dwbias, grad_norm_gain, g_lnbias, g_breduce, g_scale])
    return (
        block_out,
        grad_convolution.reshape(height, width, chans),
        grad_expand,
        grad_reduce_t,
        vectors,
        g_bexp,
    )


def back_pass(gpad, xpad, gout, dw_kernel, height, width):
    inner = gpad[3 : 3 + height, 3 : 3 + width]
    grad_in = gout.astype(jnp.float32)
    kernel_rows = []
    for i in range(7):
        row_terms = []
        for j in range(7):
            part = xpad[i : i + height, j : j + width].astype(jnp.float32)
            row_terms.append(jnp.sum(inner * part, axis=(0, 1)))
            grad_in = (
                grad_in + dw_kernel[i, j] * gpad[6 - i : 6 - i + height, 6 - j : 6 - j + width]
            )
        kernel_rows.append(jnp.stack(row_terms))
    return (grad_in.astype(jnp.bfloat16), jnp.stack(kernel_rows))


def per_device(
    feature_map,
    dw_kernel,
    dw_bias,
    layer_norm_gain,
    layer_norm_bias,
    w_expand,
    b_expand,
    w_reduce,
    b_reduce,
    layer_scale,
    cotangent,
):
    height, width = (feature_map.shape[1], feature_map.shape[2])
    xpad = extended(feature_map, (("rows", 1), ("cols", 2)), 3)[0]
    gout = cotangent[0]
    block_out, grad_convolution, gexp, gred, vectors, gbexp = front_pass(
        xpad,
        gout,
        dw_kernel,
        dw_bias,
        layer_norm_gain,
        layer_norm_bias,
        w_expand,
        b_expand,
        w_reduce,
        b_reduce,
        layer_scale,
        height,
        width,
    )
    stacked = jnp.stack([gexp, gred])
    gpad = extended(grad_convolution, (("rows", 0), ("cols", 1)), 3)
    grad_in, gker = back_pass(gpad, xpad, gout, dw_kernel, height, width)
    partial_sum = lax.psum_scatter(stacked, "rep", scatter_dimension=1, tiled=True)
    summed = lax.psum_scatter(partial_sum, ("rows", "cols"), scatter_dimension=2, tiled=True)
    gker, vectors, gbexp = lax.psum((gker, vectors, gbexp), ("rows", "cols", "rep"))
    count = lax.axis_size("rows") * height * lax.axis_size("cols") * width * lax.axis_size("rep")
    scale = 1.0 / jnp.sqrt(jnp.float32(count))
    return (
        block_out[None],
        grad_in[None],
        summed[0] * scale,
        summed[1] * scale,
        gker * scale,
        vectors * scale,
        gbexp * scale,
    )


def pack_rows(value):
    half = value.shape[0] // 2
    return jnp.concatenate([value[:half, :8], value[half:, :8]], axis=1)


def halo_source(cells, dz, dx):
    rows = cells
    if dz == -1:
        rows = cells[:4] if dx else cells[:3]
    elif dz == 1:
        rows = cells[4:] if dx else cells[5:]
    if dx == 0:
        return rows.astype(BF16)
    return pack_rows(rows[:, :8] if dx == -1 else rows[:, 8:]).astype(BF16)


def halo_target(padded, landed, dz, dx):
    if dx:
        half = landed.shape[0]
        landed = jnp.concatenate([landed[:, :8], landed[:, 8:]], axis=0)
        if dz == 1:
            landed = landed[1:]
        elif dz == -1:
            landed = landed[:3]
    rows = slice(3, 11) if dz == 0 else (slice(0, 3) if dz == 1 else slice(11, 14))
    columns = slice(8, 24) if dx == 0 else (slice(0, 8) if dx == 1 else slice(24, 32))
    padded[rows, columns, :] = landed


def halo_shape(dz, dx, chans):
    if dx == 0:
        return (3, 16, chans)
    return (4 if dz == 0 else 2, 16, chans)


def fused_kernel(
    sizes,
    scale,
    x_ref,
    gout_ref,
    dwk_ref,
    dwb_ref,
    gain_ref,
    lnb_ref,
    wexp_hbm,
    bexp_ref,
    wred_hbm,
    bred_ref,
    ls_ref,
    out_ref,
    gin_ref,
    gexp_ref,
    gred_ref,
    gker_ref,
    gvec_ref,
    gbexp_ref,
    wexp,
    wred,
    xp,
    gp,
    work,
    xhat_s,
    lhs_t,
    main0,
    main1,
    rem,
    grad_out_blocks,
    landed0,
    xsend,
    xland,
    gsend,
    gland,
    small,
    small_send,
    small_land,
    zsend,
    zland,
    final,
    keeps,
    sends,
    lands,
    wsem,
    halo_sems,
    core_sems,
    part_sems,
    small_sems,
):
    zn, xn, rn = sizes
    z, x, r = lax.axis_index("rows"), lax.axis_index("cols"), lax.axis_index("rep")
    y, c = r // 2, r % 2
    chans = x_ref.shape[-1]
    hidden = wexp.shape[1]
    core_mate = {"rows": z, "cols": x, "rep": 2 * y + 1 - c}
    y_mate = {"rows": z, "cols": x, "rep": 2 * (1 - y) + c}
    x_mate = {"rows": z, "cols": 1 - x, "rep": r}

    def z_mate(d):
        return {"rows": (z + d) % zn, "cols": x, "rep": r}

    weights = [
        pltpu.make_async_copy(wexp_hbm, wexp, wsem.at[0]),
        pltpu.make_async_copy(wred_hbm, wred, wsem.at[1]),
    ]
    for copy in weights:
        copy.start()

    def inside(a, b):
        return (a >= 0) & (a < zn) & (b >= 0) & (b < xn)

    barrier = pltpu.get_barrier_semaphore()
    greeted = jnp.int32(6)
    for mate in [core_mate, y_mate, x_mate] + [z_mate(d) for d in (1, 2, 3)]:
        pl.semaphore_signal(barrier, inc=1, device_id=mate, device_id_type=MESH)
    for dz, dx in DIRECTIONS:
        if dx == 0 or dz == 0:
            continue
        near = inside(z + dz, x + dx)

        @pl.when(near)
        def _():
            pl.semaphore_signal(
                barrier,
                inc=1,
                device_id={"rows": z + dz, "cols": x + dx, "rep": r},
                device_id_type=MESH,
            )

        greeted = greeted + near.astype(jnp.int32)

    cells = x_ref[0].astype(F32)
    for n, (dz, dx) in enumerate(DIRECTIONS):
        xsend[n][...] = halo_source(cells, dz, dx)
    xp[...] = jnp.zeros_like(xp)
    gp[...] = jnp.zeros_like(gp)
    xp[3:11, 8:24, :] = cells
    pl.semaphore_wait(barrier, greeted)

    def halo_copy(which, n):
        source, target = ((xsend, xland), (gsend, gland))[which]
        dz, dx = DIRECTIONS[n]
        return pltpu.make_async_remote_copy(
            src_ref=source[n],
            dst_ref=target[n],
            send_sem=halo_sems.at[which, 0, n],
            recv_sem=halo_sems.at[which, 1, n],
            device_id={"rows": z + dz, "cols": x + dx, "rep": r},
            device_id_type=MESH,
        )

    def halo_start(which):
        for n, (dz, dx) in enumerate(DIRECTIONS):
            pl.when(inside(z + dz, x + dx))(lambda n=n: halo_copy(which, n).start())

    def halo_finish(which, padded):
        landed = (xland, gland)[which]
        for n, (dz, dx) in enumerate(DIRECTIONS):

            @pl.when(inside(z - dz, x - dx))
            def _(n=n, dz=dz, dx=dx):
                halo_copy(which, n).wait_recv()
                halo_target(padded, landed[n][...].astype(F32), dz, dx)

    def halo_sent(which):
        for n, (dz, dx) in enumerate(DIRECTIONS):
            pl.when(inside(z + dz, x + dx))(lambda n=n: halo_copy(which, n).wait_send())

    halo_start(0)
    grad = gout_ref[0].astype(F32).reshape(-1, chans)
    scaled = grad * ls_ref[...]
    g_branch = scaled.astype(BF16)
    small[...] = jnp.zeros_like(small)
    small[52:53, :] = jnp.sum(scaled, axis=0, keepdims=True)
    weights[1].wait()
    contract_last = (((1,), (1,)), ((), ()))
    g_act = lax.dot_general(g_branch, wred[...], contract_last, preferred_element_type=F32)
    lhs_t[1] = scaled.T.astype(BF16).reshape(rn, chans // rn, 128)
    halo_finish(0, xp)

    def conv_chunk(n, carry):
        ch = pl.ds(pl.multiple_of(n * LANES, LANES), LANES)
        total = jnp.zeros((8, 16, LANES), F32) + dwb_ref[:, ch]
        for j in range(7):
            shifted = xp[:, 5 + j : 21 + j, ch]
            for i in range(7):
                total = total + dwk_ref[7 * i + j : 7 * i + j + 1, ch] * shifted[i : i + 8]
        work[:, ch] = total.reshape(128, LANES)
        return carry

    lax.fori_loop(0, chans // LANES, conv_chunk, 0)
    conv = work[...]
    centered = conv - jnp.mean(conv, axis=-1, keepdims=True)
    rstd = lax.rsqrt(jnp.mean(centered * centered, axis=-1, keepdims=True) + EPS)
    xhat = centered * rstd
    xhat_s[...] = xhat
    normed32 = xhat * gain_ref[...] + lnb_ref[...]
    normed = normed32.astype(BF16)
    lhs_t[0] = normed32.T.astype(BF16).reshape(rn, chans // rn, 128)
    weights[0].wait()
    pre = jnp.dot(normed, wexp[...], preferred_element_type=F32) + bexp_ref[...]
    cdf = 0.5 * (1.0 + lax.erf(pre * INV_ROOT_TWO))
    act32 = pre * cdf
    act = act32.astype(BF16)
    pdf = jnp.exp(-0.5 * pre * pre) * INV_ROOT_TWO_PI
    g_pre = g_act * (cdf + pre * pdf)
    bexp_sum = jnp.sum(g_pre, axis=0, keepdims=True)
    for n in range(hidden // chans):
        small[54 + n : 55 + n, :] = bexp_sum[:, n * chans : (n + 1) * chans]
    g_pre_b = g_pre.astype(BF16)

    low = lax.broadcasted_iota(jnp.int32, (128, LANES), 1) < LANES // 2
    zero = jnp.zeros((128, LANES), F32)
    for n in range(zn):
        at = 3 * LANES * n
        even, odd = slice(2 * n * LANES, (2 * n + 1) * LANES), slice((2 * n + 1) * LANES, (2 * n + 2) * LANES)
        main0[:, even] = g_pre_b[:, at : at + LANES]
        main0[:, odd] = g_pre_b[:, at + 2 * LANES : at + 3 * LANES]
        main1[:, even] = act[:, at : at + LANES]
        main1[:, odd] = act[:, at + 2 * LANES : at + 3 * LANES]
        middle = g_pre[:, at + LANES : at + 2 * LANES]
        rolled = pltpu.roll(act32[:, at + LANES : at + 2 * LANES], LANES // 2, 1)
        rem[:128, even] = jnp.where(low, middle, zero).astype(BF16)
        rem[128:, even] = jnp.where(low, zero, rolled).astype(BF16)
        rem[:128, odd] = jnp.where(low, zero, middle).astype(BF16)
        rem[128:, odd] = jnp.where(low, rolled, zero).astype(BF16)

    def products(owner):
        left0 = jnp.concatenate([lhs_t[0, owner], lhs_t[0, 2 + owner]], axis=0)
        left1 = jnp.concatenate([lhs_t[1, owner], lhs_t[1, 2 + owner]], axis=0)
        both = jnp.concatenate([left0, left1], axis=1)
        rows = chans // rn
        for k, (left, right) in enumerate(((left0, main0), (left1, main1), (both, rem))):
            for zz in range(zn):
                block = jnp.dot(
                    left, right[:, 2 * zz * LANES : (2 * zz + 2) * LANES], preferred_element_type=F32
                ).astype(BF16)
                for xx in range(xn):
                    for yy in range(2):
                        part = block[yy * rows : (yy + 1) * rows, xx * LANES : (xx + 1) * LANES]
                        grad_out_blocks[owner, :, yy, xx, zz, k] = part.reshape(-1, PIECE, LANES)

    def core_copy(p):
        return pltpu.make_async_remote_copy(
            src_ref=grad_out_blocks.at[1 - c, p],
            dst_ref=landed0.at[p],
            send_sem=core_sems.at[0, p],
            recv_sem=core_sems.at[1, p],
            device_id=core_mate,
            device_id_type=MESH,
        )

    parts = len(ORDERS)
    products(1 - c)
    for p in range(parts):
        core_copy(p).start()
    products(c)

    def place(dims, axis, index):
        return tuple(index if d == axis else slice(None) for d in dims)

    def stage_copies(p, s):
        axis = ORDERS[p][s]
        if axis == "z":
            return [
                pltpu.make_async_remote_copy(
                    src_ref=sends[p][s].at[d - 1],
                    dst_ref=lands[p][s].at[d - 1],
                    send_sem=part_sems.at[p, s, 0, d - 1],
                    recv_sem=part_sems.at[p, s, 1, d - 1],
                    device_id=z_mate(d),
                    device_id_type=MESH,
                )
                for d in (1, 2, 3)
            ]
        return [
            pltpu.make_async_remote_copy(
                src_ref=sends[p][s].at[0],
                dst_ref=lands[p][s].at[0],
                send_sem=part_sems.at[p, s, 0, 0],
                recv_sem=part_sems.at[p, s, 1, 0],
                device_id=y_mate if axis == "y" else x_mate,
                device_id_type=MESH,
            )
        ]

    def load(p, s, at):
        if s == 0:
            return grad_out_blocks[(c, p) + at].astype(F32) + landed0[(p,) + at].astype(F32)
        total = keeps[p][s - 1][at]
        for d in range(lands[p][s - 1].shape[0]):
            total = total + lands[p][s - 1][(d,) + at].astype(F32)
        return total

    def stage(p, s):
        if s == 0:
            core_copy(p).wait_recv()
        else:
            for copy in stage_copies(p, s - 1):
                copy.wait_recv()
        dims = [d for d in "yxz" if d not in ORDERS[p][:s]]
        if s == 3:
            final[:, p * PIECE : (p + 1) * PIECE, :] = load(p, s, ())
            return
        axis = ORDERS[p][s]
        copies = stage_copies(p, s)
        if axis == "z":
            for d in (1, 2, 3):
                sends[p][s][d - 1] = load(p, s, place(dims, "z", (z + d) % zn)).astype(BF16)
                copies[d - 1].start()
            keeps[p][s][...] = load(p, s, place(dims, "z", z))
        else:
            mine = y if axis == "y" else x
            sends[p][s][0] = load(p, s, place(dims, axis, 1 - mine)).astype(BF16)
            copies[0].start()
            keeps[p][s][...] = load(p, s, place(dims, axis, mine))

    for p in range(parts):
        stage(p, 0)

    g_normed = lax.dot_general(g_pre_b, wexp[...], contract_last, preferred_element_type=F32)
    xhat = xhat_s[...]
    small[50:51, :] = jnp.sum(g_normed * xhat, axis=0, keepdims=True)
    small[51:52, :] = jnp.sum(g_normed, axis=0, keepdims=True)
    gx = g_normed * gain_ref[...]
    g_conv = rstd * (
        gx
        - jnp.mean(gx, axis=-1, keepdims=True)
        - xhat * jnp.mean(gx * xhat, axis=-1, keepdims=True)
    )
    small[49:50, :] = jnp.sum(g_conv, axis=0, keepdims=True)
    g_cells = g_conv.reshape(8, 16, chans)
    for n, (dz, dx) in enumerate(DIRECTIONS):
        gsend[n][...] = halo_source(g_cells, dz, dx)
    halo_start(1)
    gp[3:11, 8:24, :] = g_cells

    branch = jnp.dot(act, wred[...], preferred_element_type=F32) + bred_ref[...]
    small[53:54, :] = jnp.sum(grad * branch, axis=0, keepdims=True)
    inner = x_ref[0].astype(F32).reshape(-1, chans)
    out_ref[0] = (inner + ls_ref[...] * branch).astype(BF16).reshape(8, 16, chans)

    def kernel_chunk(n, carry):
        ch = pl.ds(pl.multiple_of(n * LANES, LANES), LANES)
        own = gp[3:11, 8:24, ch]
        for j in range(7):
            shifted = xp[:, 5 + j : 21 + j, ch]
            for i in range(7):
                terms = jnp.sum((own * shifted[i : i + 8]).reshape(16, 8, LANES), axis=0)
                small[7 * i + j : 7 * i + j + 1, ch] = jnp.sum(terms, axis=0, keepdims=True)
        return carry

    lax.fori_loop(0, chans // LANES, kernel_chunk, 0)

    half = small.shape[0] // 2

    def small_copy(n, source, target, mate):
        return pltpu.make_async_remote_copy(
            src_ref=source,
            dst_ref=target,
            send_sem=small_sems.at[0, n],
            recv_sem=small_sems.at[1, n],
            device_id=mate,
            device_id_type=MESH,
        )

    moves = [small_copy(n, small_send.at[n], small_land.at[n], m) for n, m in enumerate((core_mate, y_mate, x_mate))]
    z_moves = [small_copy(2 + d, zsend, zland.at[d - 1], z_mate(d)) for d in (1, 2, 3)]
    other_rows = pl.ds(pl.multiple_of((1 - c) * half, half), half)
    my_rows = pl.ds(pl.multiple_of(c * half, half), half)
    small_send[0] = small[other_rows, :]
    moves[0].start()

    for p in range(parts):
        stage(p, 1)

    moves[0].wait_recv()
    small_send[1] = small[my_rows, :] + small_land[0]
    moves[1].start()

    halo_finish(1, gp)

    def input_chunk(n, carry):
        ch = pl.ds(pl.multiple_of(n * LANES, LANES), LANES)
        total = gout_ref[0, :, :, ch].astype(F32)
        for j in range(7):
            shifted = gp[:, 11 - j : 27 - j, ch]
            for i in range(7):
                total = total + dwk_ref[7 * i + j : 7 * i + j + 1, ch] * shifted[6 - i : 14 - i]
        gin_ref[0, :, :, ch] = total.astype(BF16)
        return carry

    moves[1].wait_recv()
    small_send[2] = small_send[1] + small_land[1]
    moves[2].start()
    lax.fori_loop(0, chans // LANES, input_chunk, 0)

    moves[2].wait_recv()
    zsend[...] = (small_send[2] + small_land[2]).astype(BF16)
    for move in z_moves:
        move.start()

    for p in range(parts):
        stage(p, 2)

    for move in z_moves:
        move.wait_recv()
    quarter = [zsend[...].astype(F32)] + [zland[d].astype(F32) for d in range(3)]
    total = jnp.zeros_like(quarter[0])
    for at in range(zn):
        d = (z - at) % zn
        term = quarter[0]
        for k in (1, 2, 3):
            term = jnp.where(d == k, quarter[k], term)
        total = total + term
    small_send[3] = total * scale
    last = small_copy(6, small_send.at[3], small_land.at[3], core_mate)
    last.start()

    for p in range(parts):
        stage(p, 3)
    blocks = final[...] * scale
    wide = LANES + LANES // 2
    m0, m1, mixed = blocks[0], blocks[1], blocks[2]
    first, second = mixed[:, : LANES // 2], mixed[:, LANES // 2 :]

    @pl.when(x == 0)
    def _():
        gexp_ref[:, :LANES] = m0
        gexp_ref[:, LANES:wide] = first
        gred_ref[:, :LANES] = m1
        gred_ref[:, LANES:wide] = second

    @pl.when(x == 1)
    def _():
        gexp_ref[...] = jnp.concatenate([second, m0], axis=1)
        gred_ref[...] = jnp.concatenate([first, m1], axis=1)

    last.wait_recv()
    small[my_rows, :] = small_send[3]
    small[other_rows, :] = small_land[3]
    for i in range(7):
        gker_ref[i] = small[7 * i : 7 * i + 7, :]
    gvec_ref[...] = small[49:54, :]
    for n in range(hidden // chans):
        gbexp_ref[:, n * chans : (n + 1) * chans] = small[54 + n : 55 + n, :]

    halo_sent(0)
    halo_sent(1)
    for p in range(parts):
        core_copy(p).wait_send()
        for s in range(3):
            for copy in stage_copies(p, s):
                copy.wait_send()
    for move in moves + z_moves + [last]:
        move.wait_send()


def fused(mesh_sizes, *args):
    (
        feature_map,
        dw_kernel,
        dw_bias,
        layer_norm_gain,
        layer_norm_bias,
        w_expand,
        b_expand,
        w_reduce,
        b_reduce,
        layer_scale,
        cotangent,
    ) = args
    zn, xn, rn = mesh_sizes
    _, height, width, chans = feature_map.shape
    hidden = w_expand.shape[1]
    pixels = height * width * zn * xn * rn
    scale = float(pixels) ** -0.5
    vmem = pl.BlockSpec(memory_space=pltpu.VMEM)
    anywhere = pl.BlockSpec(memory_space=pl.ANY)
    parts = len(ORDERS)
    block = (3, PIECE, LANES)
    keeps, sends, lands = [], [], []
    for order in ORDERS:
        keeps.append([])
        sends.append([])
        lands.append([])
        for s in range(3):
            left = tuple(SIZES[d] for d in "yxz" if d not in order[: s + 1])
            copies = 3 if order[s] == "z" else 1
            keeps[-1].append(pltpu.VMEM(left + block, F32))
            sends[-1].append(pltpu.VMEM((copies,) + left + block, BF16))
            lands[-1].append(pltpu.VMEM((copies,) + left + block, BF16))
    halos = [pltpu.VMEM(halo_shape(dz, dx, chans), BF16) for dz, dx in DIRECTIONS]
    scratch = dict(
        wexp=pltpu.VMEM(w_expand.shape, BF16),
        wred=pltpu.VMEM(w_reduce.shape, BF16),
        xp=pltpu.VMEM((14, 32, chans), F32),
        gp=pltpu.VMEM((14, 32, chans), F32),
        work=pltpu.VMEM((128, chans), F32),
        xhat_s=pltpu.VMEM((128, chans), F32),
        lhs_t=pltpu.VMEM((2, rn, chans // rn, 128), BF16),
        main0=pltpu.VMEM((128, 2 * zn * LANES), BF16),
        main1=pltpu.VMEM((128, 2 * zn * LANES), BF16),
        rem=pltpu.VMEM((256, 2 * zn * LANES), BF16),
        grad_out_blocks=pltpu.VMEM((2, parts, 2, xn, zn) + block, BF16),
        landed0=pltpu.VMEM((parts, 2, xn, zn) + block, BF16),
        xsend=list(halos),
        xland=list(halos),
        gsend=list(halos),
        gland=list(halos),
        small=pltpu.VMEM((64, chans), F32),
        small_send=pltpu.VMEM((4, 32, chans), F32),
        small_land=pltpu.VMEM((4, 32, chans), F32),
        zsend=pltpu.VMEM((32, chans), BF16),
        zland=pltpu.VMEM((3, 32, chans), BF16),
        final=pltpu.VMEM((3, parts * PIECE, LANES), F32),
        keeps=keeps,
        sends=sends,
        lands=lands,
        wsem=pltpu.SemaphoreType.DMA((2,)),
        halo_sems=pltpu.SemaphoreType.DMA((2, 2, 8)),
        core_sems=pltpu.SemaphoreType.DMA((2, parts)),
        part_sems=pltpu.SemaphoreType.DMA((parts, 3, 2, 3)),
        small_sems=pltpu.SemaphoreType.DMA((2, 7)),
    )
    rows, columns = chans // rn, hidden // (zn * xn)
    outs = pl.pallas_call(
        functools.partial(fused_kernel, mesh_sizes, scale),
        out_shape=[
            jax.ShapeDtypeStruct(feature_map.shape, BF16),
            jax.ShapeDtypeStruct(feature_map.shape, BF16),
            jax.ShapeDtypeStruct((rows, columns), F32),
            jax.ShapeDtypeStruct((rows, columns), F32),
            jax.ShapeDtypeStruct(dw_kernel.shape, F32),
            jax.ShapeDtypeStruct((5, chans), F32),
            jax.ShapeDtypeStruct((1, hidden), F32),
        ],
        in_specs=[vmem] * 6 + [anywhere, vmem, anywhere, vmem, vmem],
        out_specs=[vmem] * 7,
        scratch_shapes=list(scratch.values()),
        compiler_params=pltpu.CompilerParams(
            collective_id=0, has_side_effects=True, vmem_limit_bytes=48 * 1024 * 1024
        ),
    )(
        feature_map,
        cotangent,
        dw_kernel.reshape(49, chans),
        dw_bias.reshape(1, -1),
        layer_norm_gain.reshape(1, -1),
        layer_norm_bias.reshape(1, -1),
        w_expand,
        b_expand.reshape(1, -1),
        w_reduce,
        b_reduce.reshape(1, -1),
        layer_scale.reshape(1, -1),
    )
    return tuple(outs[:6]) + (outs[6].reshape(-1),)


def fits(sizes):
    return sizes == (4, 2, 4)


def solution(mesh):
    in_specs = (
        P("rep", "rows", "cols", None),
        P(),
        P(),
        P(),
        P(),
        P(),
        P(),
        P(),
        P(),
        P(),
        P("rep", "rows", "cols", None),
    )
    out_specs = (
        P("rep", "rows", "cols", None),
        P("rep", "rows", "cols", None),
        P("rep", ("rows", "cols")),
        P("rep", ("rows", "cols")),
        P(),
        P(),
        P(),
    )
    sizes = tuple(mesh.shape[a] for a in ("rows", "cols", "rep"))
    body = functools.partial(fused, sizes) if fits(sizes) else per_device
    return jax.shard_map(
        body, mesh=mesh, in_specs=in_specs, out_specs=out_specs, check_vma=False
    )
```

```python
import functools

import jax
import jax.numpy as jnp
from jax import lax
from jax.experimental import pallas as pl
from jax.experimental.pallas import tpu as pltpu
from jax.sharding import PartitionSpec as P

MESH = pl.DeviceIdType.MESH
F32, BF16 = jnp.float32, jnp.bfloat16
LANES = 128
PIECE = 16
VMEM_BYTES = 64 * 1024 * 1024
ORDERS = ("yxz", "xyz", "zyx", "xyz", "yxz", "xyz")
DIRECTIONS = ((-1, 0), (1, 0), (0, -1), (0, 1), (-1, -1), (-1, 1), (1, -1), (1, 1))
SIZES = {"y": 2, "x": 2, "z": 4}

EPS = 1e-06
INV_ROOT_TWO = 0.7071067811865476
INV_ROOT_TWO_PI = 0.3989422804014327


def extended(cells, sides, width):
    for axis, dim in sides:
        count = lax.axis_size(axis)
        ends = count - 1
        head = lax.slice_in_dim(cells, 0, width, axis=dim)
        tail = lax.slice_in_dim(cells, cells.shape[dim] - width, cells.shape[dim], axis=dim)
        cells = jnp.concatenate(
            [
                lax.ppermute(tail, axis, [(i, (i + 1) % count) for i in range(ends)]),
                cells,
                lax.ppermute(head, axis, [((i + 1) % count, i) for i in range(ends)]),
            ],
            axis=dim,
        )
    return cells


def depthwise(padded, kernel, height, width):
    total = jnp.zeros((height, width, padded.shape[-1]), jnp.float32)
    for i in range(7):
        for j in range(7):
            total = total + kernel[i, j] * padded[i : i + height, j : j + width].astype(jnp.float32)
    return total


def front_pass(
    xpad,
    gout,
    dw_kernel,
    dw_bias,
    layer_norm_gain,
    layer_norm_bias,
    w_expand,
    b_expand,
    w_reduce,
    b_reduce,
    layer_scale,
    height,
    width,
):
    chans = xpad.shape[-1]
    conv = depthwise(xpad, dw_kernel, height, width) + dw_bias
    flat = conv.reshape(-1, chans)
    centered_input = flat - jnp.mean(flat, axis=-1, keepdims=True)
    inverse_deviation = lax.rsqrt(
        jnp.mean(centered_input * centered_input, axis=-1, keepdims=True) + EPS
    )
    standardized_input = centered_input * inverse_deviation
    normalized_rows = (standardized_input * layer_norm_gain + layer_norm_bias).astype(jnp.bfloat16)
    pre = jnp.dot(normalized_rows, w_expand, preferred_element_type=jnp.float32) + b_expand
    cdf = 0.5 * (1.0 + lax.erf(pre * INV_ROOT_TWO))
    act = (pre * cdf).astype(jnp.bfloat16)
    branch = jnp.dot(act, w_reduce, preferred_element_type=jnp.float32) + b_reduce
    inner = xpad[3 : 3 + height, 3 : 3 + width].reshape(-1, chans).astype(jnp.float32)
    block_out = (inner + layer_scale * branch).astype(jnp.bfloat16).reshape(height, width, chans)
    grad = gout.reshape(-1, chans).astype(jnp.float32)
    scaled = grad * layer_scale
    g_branch = scaled.astype(jnp.bfloat16)
    g_scale = jnp.sum(grad * branch, axis=0)
    g_breduce = jnp.sum(scaled, axis=0)
    grad_reduce_t = lax.dot_general(
        g_branch, act, (((0,), (0,)), ((), ())), preferred_element_type=jnp.float32
    )
    g_act = lax.dot_general(
        g_branch, w_reduce, (((1,), (1,)), ((), ())), preferred_element_type=jnp.float32
    )
    pdf = jnp.exp(-0.5 * pre * pre) * INV_ROOT_TWO_PI
    g_pre = g_act * (cdf + pre * pdf)
    g_bexp = jnp.sum(g_pre, axis=0)
    g_pre_b = g_pre.astype(jnp.bfloat16)
    grad_expand = lax.dot_general(
        normalized_rows, g_pre_b, (((0,), (0,)), ((), ())), preferred_element_type=jnp.float32
    )
    grad_normalized = lax.dot_general(
        g_pre_b, w_expand, (((1,), (1,)), ((), ())), preferred_element_type=jnp.float32
    )
    grad_norm_gain = jnp.sum(grad_normalized * standardized_input, axis=0)
    g_lnbias = jnp.sum(grad_normalized, axis=0)
    scaled_grad_input = grad_normalized * layer_norm_gain
    grad_convolution = inverse_deviation * (
        scaled_grad_input
        - jnp.mean(scaled_grad_input, axis=-1, keepdims=True)
        - standardized_input
        * jnp.mean(scaled_grad_input * standardized_input, axis=-1, keepdims=True)
    )
    g_dwbias = jnp.sum(grad_convolution, axis=0)
    vectors = jnp.stack([g_dwbias, grad_norm_gain, g_lnbias, g_breduce, g_scale])
    return (
        block_out,
        grad_convolution.reshape(height, width, chans),
        grad_expand,
        grad_reduce_t,
        vectors,
        g_bexp,
    )


def back_pass(gpad, xpad, gout, dw_kernel, height, width):
    inner = gpad[3 : 3 + height, 3 : 3 + width]
    grad_in = gout.astype(jnp.float32)
    kernel_rows = []
    for i in range(7):
        row_terms = []
        for j in range(7):
            part = xpad[i : i + height, j : j + width].astype(jnp.float32)
            row_terms.append(jnp.sum(inner * part, axis=(0, 1)))
            grad_in = (
                grad_in + dw_kernel[i, j] * gpad[6 - i : 6 - i + height, 6 - j : 6 - j + width]
            )
        kernel_rows.append(jnp.stack(row_terms))
    return (grad_in.astype(jnp.bfloat16), jnp.stack(kernel_rows))


def per_device(
    feature_map,
    dw_kernel,
    dw_bias,
    layer_norm_gain,
    layer_norm_bias,
    w_expand,
    b_expand,
    w_reduce,
    b_reduce,
    layer_scale,
    cotangent,
):
    height, width = (feature_map.shape[1], feature_map.shape[2])
    xpad = extended(feature_map, (("rows", 1), ("cols", 2)), 3)[0]
    gout = cotangent[0]
    block_out, grad_convolution, gexp, gred, vectors, gbexp = front_pass(
        xpad,
        gout,
        dw_kernel,
        dw_bias,
        layer_norm_gain,
        layer_norm_bias,
        w_expand,
        b_expand,
        w_reduce,
        b_reduce,
        layer_scale,
        height,
        width,
    )
    stacked = jnp.stack([gexp, gred])
    gpad = extended(grad_convolution, (("rows", 0), ("cols", 1)), 3)
    grad_in, gker = back_pass(gpad, xpad, gout, dw_kernel, height, width)
    partial_sum = lax.psum_scatter(stacked, "rep", scatter_dimension=1, tiled=True)
    summed = lax.psum_scatter(partial_sum, ("rows", "cols"), scatter_dimension=2, tiled=True)
    gker, vectors, gbexp = lax.psum((gker, vectors, gbexp), ("rows", "cols", "rep"))
    count = lax.axis_size("rows") * height * lax.axis_size("cols") * width * lax.axis_size("rep")
    scale = 1.0 / jnp.sqrt(jnp.float32(count))
    return (
        block_out[None],
        grad_in[None],
        summed[0] * scale,
        summed[1] * scale,
        gker * scale,
        vectors * scale,
        gbexp * scale,
    )


def pack_rows(value):
    half = value.shape[0] // 2
    return jnp.concatenate([value[:half, :8], value[half:, :8]], axis=1)


def halo_source(cells, dz, dx):
    rows = cells
    if dz == -1:
        rows = cells[:4] if dx else cells[:3]
    elif dz == 1:
        rows = cells[4:] if dx else cells[5:]
    if dx == 0:
        return rows.astype(BF16)
    return pack_rows(rows[:, :8] if dx == -1 else rows[:, 8:]).astype(BF16)


def halo_target(padded, landed, dz, dx):
    if dx:
        half = landed.shape[0]
        landed = jnp.concatenate([landed[:, :8], landed[:, 8:]], axis=0)
        if dz == 1:
            landed = landed[1:]
        elif dz == -1:
            landed = landed[:3]
    rows = slice(3, 11) if dz == 0 else (slice(0, 3) if dz == 1 else slice(11, 14))
    columns = slice(8, 24) if dx == 0 else (slice(0, 8) if dx == 1 else slice(24, 32))
    padded[rows, columns, :] = landed


def halo_shape(dz, dx, chans):
    if dx == 0:
        return (3, 16, chans)
    return (4 if dz == 0 else 2, 16, chans)


def fused_kernel(
    sizes,
    scale,
    x_hbm,
    gout_hbm,
    dwk_hbm,
    dwb_hbm,
    gain_hbm,
    lnb_hbm,
    wexp_hbm,
    bexp_hbm,
    wred_hbm,
    bred_hbm,
    ls_hbm,
    out_ref,
    gin_ref,
    gexp_ref,
    gred_ref,
    gker_ref,
    gvec_ref,
    gbexp_ref,
    x_ref,
    gout_ref,
    dwk_ref,
    dwb_1d,
    gain_1d,
    lnb_1d,
    wexp,
    bexp_1d,
    wred,
    bred_1d,
    ls_1d,
    bexp_ref,
    pre_s,
    gact_s,
    xp,
    gp,
    work,
    xhat_s,
    lhs_t,
    act_s,
    gpre_s,
    main0,
    main1,
    rem,
    grad_out_blocks,
    landed0,
    xsend,
    xland,
    gsend,
    gland,
    small,
    small_send,
    small_land,
    zsend,
    zland,
    final,
    keeps,
    sends,
    lands,
    wsem,
    halo_sems,
    core_sems,
    part_sems,
    small_sems,
):
    zn, xn, rn = sizes
    z, x, r = lax.axis_index("rows"), lax.axis_index("cols"), lax.axis_index("rep")
    y, c = r // 2, r % 2
    chans = x_ref.shape[-1]
    hidden = wexp.shape[1]
    core_mate = {"rows": z, "cols": x, "rep": 2 * y + 1 - c}
    y_mate = {"rows": z, "cols": x, "rep": 2 * (1 - y) + c}
    x_mate = {"rows": z, "cols": 1 - x, "rep": r}

    def z_mate(d):
        return {"rows": (z + d) % zn, "cols": x, "rep": r}

    fetches = [
        pltpu.make_async_copy(source, target, wsem.at[n])
        for n, (source, target) in enumerate(
            (
                (x_hbm, x_ref),
                (gout_hbm, gout_ref),
                (ls_hbm, ls_1d),
                (wred_hbm, wred),
                (dwb_hbm, dwb_1d),
                (dwk_hbm, dwk_ref),
                (gain_hbm, gain_1d),
                (lnb_hbm, lnb_1d),
                (bexp_hbm, bexp_1d),
                (bred_hbm, bred_1d),
                (wexp_hbm, wexp),
            )
        )
    ]
    for copy in fetches:
        copy.start()

    def inside(a, b):
        return (a >= 0) & (a < zn) & (b >= 0) & (b < xn)

    barrier = pltpu.get_barrier_semaphore()
    greeted = jnp.int32(6)
    for mate in [core_mate, y_mate, x_mate] + [z_mate(d) for d in (1, 2, 3)]:
        pl.semaphore_signal(barrier, inc=1, device_id=mate, device_id_type=MESH)
    for dz, dx in DIRECTIONS:
        if dx == 0 or dz == 0:
            continue
        near = inside(z + dz, x + dx)

        @pl.when(near)
        def _():
            pl.semaphore_signal(
                barrier,
                inc=1,
                device_id={"rows": z + dz, "cols": x + dx, "rep": r},
                device_id_type=MESH,
            )

        greeted = greeted + near.astype(jnp.int32)

    xp[...] = jnp.zeros_like(xp)
    gp[...] = jnp.zeros_like(gp)
    small[...] = jnp.zeros_like(small)
    fetches[0].wait()
    cells = x_ref[0].astype(F32)
    for n, (dz, dx) in enumerate(DIRECTIONS):
        xsend[n][...] = halo_source(cells, dz, dx)
    xp[3:11, 8:24, :] = cells
    pl.semaphore_wait(barrier, greeted)

    def halo_copy(which, n):
        source, target = ((xsend, xland), (gsend, gland))[which]
        dz, dx = DIRECTIONS[n]
        return pltpu.make_async_remote_copy(
            src_ref=source[n],
            dst_ref=target[n],
            send_sem=halo_sems.at[which, 0, n],
            recv_sem=halo_sems.at[which, 1, n],
            device_id={"rows": z + dz, "cols": x + dx, "rep": r},
            device_id_type=MESH,
        )

    def halo_start(which):
        for n, (dz, dx) in enumerate(DIRECTIONS):
            pl.when(inside(z + dz, x + dx))(lambda n=n: halo_copy(which, n).start())

    def halo_finish(which, padded):
        landed = (xland, gland)[which]
        for n, (dz, dx) in enumerate(DIRECTIONS):

            @pl.when(inside(z - dz, x - dx))
            def _(n=n, dz=dz, dx=dx):
                halo_copy(which, n).wait_recv()
                halo_target(padded, landed[n][...].astype(F32), dz, dx)

    def halo_sent(which):
        for n, (dz, dx) in enumerate(DIRECTIONS):
            pl.when(inside(z + dz, x + dx))(lambda n=n: halo_copy(which, n).wait_send())

    halo_start(0)
    for copy in fetches[1:10]:
        copy.wait()

    def row(ref):
        return ref[...].reshape(1, -1)

    layer_scale, gain = row(ls_1d), row(gain_1d)
    bexp_ref[...] = row(bexp_1d)
    grad = gout_ref[0].astype(F32).reshape(-1, chans)
    scaled = grad * layer_scale
    g_branch = scaled.astype(BF16)
    small[52:53, :] = jnp.sum(scaled, axis=0, keepdims=True)
    contract_last = (((1,), (1,)), ((), ()))
    gact_s[...] = lax.dot_general(g_branch, wred[...], contract_last, preferred_element_type=F32)
    lhs_t[1] = scaled.T.astype(BF16).reshape(rn, chans // rn, 128)
    bias = row(dwb_1d)
    work[...] = jnp.broadcast_to(bias, work.shape)
    halo_finish(0, xp)

    def conv_chunk(n, carry):
        ch = pl.ds(pl.multiple_of(n * LANES, LANES), LANES)
        total = work[:, ch].reshape(8, 16, LANES)
        for j in range(7):
            shifted = xp[:, 5 + j : 21 + j, ch]
            for i in range(7):
                total = total + dwk_ref[i, j : j + 1, ch] * shifted[i : i + 8]
        work[:, ch] = total.reshape(128, LANES)
        return carry

    lax.fori_loop(0, chans // LANES, conv_chunk, 0)
    conv = work[...]
    centered = conv - jnp.mean(conv, axis=-1, keepdims=True)
    rstd = lax.rsqrt(jnp.mean(centered * centered, axis=-1, keepdims=True) + EPS)
    xhat = centered * rstd
    xhat_s[...] = xhat
    normed32 = xhat * gain + row(lnb_1d)
    normed = normed32.astype(BF16)
    lhs_t[0] = normed32.T.astype(BF16).reshape(rn, chans // rn, 128)
    fetches[10].wait()
    pre_s[...] = jnp.dot(normed, wexp[...], preferred_element_type=F32)

    lower = lax.broadcasted_iota(jnp.int32, (64, LANES), 1) < LANES // 2
    zero = jnp.zeros((64, LANES), F32)

    def hidden_pair(n, carry):
        here = pl.multiple_of(n * 3 * LANES, LANES)
        even = pl.ds(pl.multiple_of(2 * n * LANES, LANES), LANES)
        odd = pl.ds(pl.multiple_of(2 * n * LANES + LANES, LANES), LANES)
        sums = []
        for group in range(3):
            ch = pl.ds(pl.multiple_of(here + group * LANES, LANES), LANES)
            sums.append(jnp.zeros((1, LANES), F32))
            for top in (0, 64):
                rows = slice(top, top + 64)
                after = slice(128 + top, 192 + top)
                pre = pre_s[rows, ch] + bexp_ref[:, ch]
                cdf = 0.5 * (1.0 + lax.erf(pre * INV_ROOT_TWO))
                act = pre * cdf
                pdf = jnp.exp(-0.5 * pre * pre) * INV_ROOT_TWO_PI
                g_pre = gact_s[rows, ch] * (cdf + pre * pdf)
                sums[-1] = sums[-1] + jnp.sum(g_pre, axis=0, keepdims=True)
                act_s[rows, ch] = act.astype(BF16)
                gpre_s[rows, ch] = g_pre.astype(BF16)
                if group == 1:
                    rolled = pltpu.roll(act, LANES // 2, 1)
                    rem[rows, even] = jnp.where(lower, g_pre, zero).astype(BF16)
                    rem[after, even] = jnp.where(lower, zero, rolled).astype(BF16)
                    rem[rows, odd] = jnp.where(lower, zero, g_pre).astype(BF16)
                    rem[after, odd] = jnp.where(lower, rolled, zero).astype(BF16)
                else:
                    to = odd if group else even
                    main0[rows, to] = g_pre.astype(BF16)
                    main1[rows, to] = act.astype(BF16)
        bexp_ref[:, pl.ds(here, 3 * LANES)] = jnp.concatenate(sums, axis=1)
        return carry

    lax.fori_loop(0, zn, hidden_pair, 0)
    for n in range(hidden // chans):
        small[54 + n : 55 + n, :] = bexp_ref[:, n * chans : (n + 1) * chans]

    def products(owner):
        left0 = jnp.concatenate([lhs_t[0, owner], lhs_t[0, 2 + owner]], axis=0)
        left1 = jnp.concatenate([lhs_t[1, owner], lhs_t[1, 2 + owner]], axis=0)
        both = jnp.concatenate([left0, left1], axis=1)
        rows = chans // rn
        for k, (left, right) in enumerate(((left0, main0), (left1, main1), (both, rem))):
            for zz in range(zn):
                block = jnp.dot(
                    left, right[:, 2 * zz * LANES : (2 * zz + 2) * LANES], preferred_element_type=F32
                ).astype(BF16)
                for xx in range(xn):
                    for yy in range(2):
                        part = block[yy * rows : (yy + 1) * rows, xx * LANES : (xx + 1) * LANES]
                        grad_out_blocks[owner, :, yy, xx, zz, k] = part.reshape(-1, PIECE, LANES)

    def core_copy(p):
        return pltpu.make_async_remote_copy(
            src_ref=grad_out_blocks.at[1 - c, p],
            dst_ref=landed0.at[p],
            send_sem=core_sems.at[0, p],
            recv_sem=core_sems.at[1, p],
            device_id=core_mate,
            device_id_type=MESH,
        )

    parts = len(ORDERS)
    products(1 - c)
    for p in range(parts):
        core_copy(p).start()
    products(c)

    def place(dims, axis, index):
        return tuple(index if d == axis else slice(None) for d in dims)

    def stage_copies(p, s):
        axis = ORDERS[p][s]
        if axis == "z":
            return [
                pltpu.make_async_remote_copy(
                    src_ref=sends[p][s].at[d - 1],
                    dst_ref=lands[p][s].at[d - 1],
                    send_sem=part_sems.at[p, s, 0, d - 1],
                    recv_sem=part_sems.at[p, s, 1, d - 1],
                    device_id=z_mate(d),
                    device_id_type=MESH,
                )
                for d in (1, 2, 3)
            ]
        return [
            pltpu.make_async_remote_copy(
                src_ref=sends[p][s].at[0],
                dst_ref=lands[p][s].at[0],
                send_sem=part_sems.at[p, s, 0, 0],
                recv_sem=part_sems.at[p, s, 1, 0],
                device_id=y_mate if axis == "y" else x_mate,
                device_id_type=MESH,
            )
        ]

    def load(p, s, at):
        if s == 0:
            return grad_out_blocks[(c, p) + at].astype(F32) + landed0[(p,) + at].astype(F32)
        total = keeps[p][s - 1][at]
        for d in range(lands[p][s - 1].shape[0]):
            total = total + lands[p][s - 1][(d,) + at].astype(F32)
        return total

    def stage(p, s):
        if s == 0:
            core_copy(p).wait_recv()
        else:
            for copy in stage_copies(p, s - 1):
                copy.wait_recv()
        dims = [d for d in "yxz" if d not in ORDERS[p][:s]]
        if s == 3:
            final[:, p * PIECE : (p + 1) * PIECE, :] = load(p, s, ())
            return
        axis = ORDERS[p][s]
        copies = stage_copies(p, s)
        if axis == "z":
            for d in (1, 2, 3):
                sends[p][s][d - 1] = load(p, s, place(dims, "z", (z + d) % zn)).astype(BF16)
                copies[d - 1].start()
            keeps[p][s][...] = load(p, s, place(dims, "z", z))
        else:
            mine = y if axis == "y" else x
            sends[p][s][0] = load(p, s, place(dims, axis, 1 - mine)).astype(BF16)
            copies[0].start()
            keeps[p][s][...] = load(p, s, place(dims, axis, mine))

    for p in range(parts):
        stage(p, 0)

    g_normed = lax.dot_general(gpre_s[...], wexp[...], contract_last, preferred_element_type=F32)
    xhat = xhat_s[...]
    small[50:51, :] = jnp.sum(g_normed * xhat, axis=0, keepdims=True)
    small[51:52, :] = jnp.sum(g_normed, axis=0, keepdims=True)
    gx = g_normed * gain
    g_conv = rstd * (
        gx
        - jnp.mean(gx, axis=-1, keepdims=True)
        - xhat * jnp.mean(gx * xhat, axis=-1, keepdims=True)
    )
    small[49:50, :] = jnp.sum(g_conv, axis=0, keepdims=True)
    g_cells = g_conv.reshape(8, 16, chans)
    for n, (dz, dx) in enumerate(DIRECTIONS):
        gsend[n][...] = halo_source(g_cells, dz, dx)
    halo_start(1)
    gp[3:11, 8:24, :] = g_cells
    for p in range(3):
        stage(p, 1)

    branch = jnp.dot(act_s[...], wred[...], preferred_element_type=F32) + row(bred_1d)
    small[53:54, :] = jnp.sum(grad * branch, axis=0, keepdims=True)
    inner = x_ref[0].astype(F32).reshape(-1, chans)
    out_ref[0] = (inner + layer_scale * branch).astype(BF16).reshape(8, 16, chans)

    def kernel_chunk(n, carry):
        ch = pl.ds(pl.multiple_of(n * LANES, LANES), LANES)
        own = gp[3:11, 8:24, ch]
        for j in range(7):
            shifted = xp[:, 5 + j : 21 + j, ch]
            for i in range(7):
                terms = jnp.sum((own * shifted[i : i + 8]).reshape(16, 8, LANES), axis=0)
                small[7 * i + j : 7 * i + j + 1, ch] = jnp.sum(terms, axis=0, keepdims=True)
        return carry

    lax.fori_loop(0, chans // LANES, kernel_chunk, 0)

    half = small.shape[0] // 2

    def small_copy(n, source, target, mate):
        return pltpu.make_async_remote_copy(
            src_ref=source,
            dst_ref=target,
            send_sem=small_sems.at[0, n],
            recv_sem=small_sems.at[1, n],
            device_id=mate,
            device_id_type=MESH,
        )

    moves = [small_copy(n, small_send.at[n], small_land.at[n], m) for n, m in enumerate((core_mate, y_mate, x_mate))]
    z_moves = [small_copy(2 + d, zsend, zland.at[d - 1], z_mate(d)) for d in (1, 2, 3)]
    other_rows = pl.ds(pl.multiple_of((1 - c) * half, half), half)
    my_rows = pl.ds(pl.multiple_of(c * half, half), half)
    small_send[0] = small[other_rows, :]
    moves[0].start()

    for p in range(3, parts):
        stage(p, 1)

    moves[0].wait_recv()
    small_send[1] = small[my_rows, :] + small_land[0]
    moves[1].start()
    for p in range(3):
        stage(p, 2)

    halo_finish(1, gp)

    def input_chunk(n, carry):
        ch = pl.ds(pl.multiple_of(n * LANES, LANES), LANES)
        total = gout_ref[0, :, :, ch].astype(F32)
        for j in range(7):
            shifted = gp[:, 11 - j : 27 - j, ch]
            for i in range(7):
                total = total + dwk_ref[i, j : j + 1, ch] * shifted[6 - i : 14 - i]
        gin_ref[0, :, :, ch] = total.astype(BF16)
        return carry

    moves[1].wait_recv()
    small_send[2] = small_send[1] + small_land[1]
    moves[2].start()
    lax.fori_loop(0, chans // LANES, input_chunk, 0)

    moves[2].wait_recv()
    zsend[...] = (small_send[2] + small_land[2]).astype(BF16)
    for move in z_moves:
        move.start()

    for p in range(3, parts):
        stage(p, 2)

    for move in z_moves:
        move.wait_recv()
    quarter = [zsend[...].astype(F32)] + [zland[d].astype(F32) for d in range(3)]
    total = jnp.zeros_like(quarter[0])
    for at in range(zn):
        d = (z - at) % zn
        term = quarter[0]
        for k in (1, 2, 3):
            term = jnp.where(d == k, quarter[k], term)
        total = total + term
    small_send[3] = total * scale
    last = small_copy(6, small_send.at[3], small_land.at[3], core_mate)
    last.start()

    for p in range(parts):
        stage(p, 3)
    blocks = final[...] * scale
    wide = LANES + LANES // 2
    m0, m1, mixed = blocks[0], blocks[1], blocks[2]
    first, second = mixed[:, : LANES // 2], mixed[:, LANES // 2 :]

    @pl.when(x == 0)
    def _():
        gexp_ref[:, :LANES] = m0
        gexp_ref[:, LANES:wide] = first
        gred_ref[:, :LANES] = m1
        gred_ref[:, LANES:wide] = second

    @pl.when(x == 1)
    def _():
        gexp_ref[...] = jnp.concatenate([second, m0], axis=1)
        gred_ref[...] = jnp.concatenate([first, m1], axis=1)

    last.wait_recv()
    small[my_rows, :] = small_send[3]
    small[other_rows, :] = small_land[3]
    for i in range(7):
        gker_ref[i] = small[7 * i : 7 * i + 7, :]
    gvec_ref[...] = small[49:54, :]
    for n in range(hidden // chans):
        bexp_ref[:, n * chans : (n + 1) * chans] = small[54 + n : 55 + n, :]
    gbexp_ref[...] = bexp_ref[...].reshape(-1)

    halo_sent(0)
    halo_sent(1)
    for p in range(parts):
        core_copy(p).wait_send()
        for s in range(3):
            for copy in stage_copies(p, s):
                copy.wait_send()
    for move in moves + z_moves + [last]:
        move.wait_send()


def fused(mesh_sizes, *args):
    (
        feature_map,
        dw_kernel,
        dw_bias,
        layer_norm_gain,
        layer_norm_bias,
        w_expand,
        b_expand,
        w_reduce,
        b_reduce,
        layer_scale,
        cotangent,
    ) = args
    zn, xn, rn = mesh_sizes
    _, height, width, chans = feature_map.shape
    hidden = w_expand.shape[1]
    pixels = height * width * zn * xn * rn
    scale = float(pixels) ** -0.5
    vmem = pl.BlockSpec(memory_space=pltpu.VMEM)
    hbm = pl.BlockSpec(memory_space=pltpu.HBM)
    parts = len(ORDERS)
    block = (3, PIECE, LANES)
    keeps, sends, lands = [], [], []
    for order in ORDERS:
        keeps.append([])
        sends.append([])
        lands.append([])
        for s in range(3):
            left = tuple(SIZES[d] for d in "yxz" if d not in order[: s + 1])
            copies = 3 if order[s] == "z" else 1
            keeps[-1].append(pltpu.VMEM(left + block, F32))
            sends[-1].append(pltpu.VMEM((copies,) + left + block, BF16))
            lands[-1].append(pltpu.VMEM((copies,) + left + block, BF16))
    halos = [pltpu.VMEM(halo_shape(dz, dx, chans), BF16) for dz, dx in DIRECTIONS]
    scratch = dict(
        x_ref=pltpu.VMEM(feature_map.shape, BF16),
        gout_ref=pltpu.VMEM(cotangent.shape, BF16),
        dwk_ref=pltpu.VMEM(dw_kernel.shape, F32),
        dwb_1d=pltpu.VMEM((chans,), F32),
        gain_1d=pltpu.VMEM((chans,), F32),
        lnb_1d=pltpu.VMEM((chans,), F32),
        wexp=pltpu.VMEM(w_expand.shape, BF16),
        bexp_1d=pltpu.VMEM((hidden,), F32),
        wred=pltpu.VMEM(w_reduce.shape, BF16),
        bred_1d=pltpu.VMEM((chans,), F32),
        ls_1d=pltpu.VMEM((chans,), F32),
        bexp_ref=pltpu.VMEM((1, hidden), F32),
        pre_s=pltpu.VMEM((128, hidden), F32),
        gact_s=pltpu.VMEM((128, hidden), F32),
        xp=pltpu.VMEM((14, 32, chans), F32),
        gp=pltpu.VMEM((14, 32, chans), F32),
        work=pltpu.VMEM((128, chans), F32),
        xhat_s=pltpu.VMEM((128, chans), F32),
        lhs_t=pltpu.VMEM((2, rn, chans // rn, 128), BF16),
        act_s=pltpu.VMEM((128, hidden), BF16),
        gpre_s=pltpu.VMEM((128, hidden), BF16),
        main0=pltpu.VMEM((128, 2 * zn * LANES), BF16),
        main1=pltpu.VMEM((128, 2 * zn * LANES), BF16),
        rem=pltpu.VMEM((256, 2 * zn * LANES), BF16),
        grad_out_blocks=pltpu.VMEM((2, parts, 2, xn, zn) + block, BF16),
        landed0=pltpu.VMEM((parts, 2, xn, zn) + block, BF16),
        xsend=list(halos),
        xland=list(halos),
        gsend=list(halos),
        gland=list(halos),
        small=pltpu.VMEM((64, chans), F32),
        small_send=pltpu.VMEM((4, 32, chans), F32),
        small_land=pltpu.VMEM((4, 32, chans), F32),
        zsend=pltpu.VMEM((32, chans), BF16),
        zland=pltpu.VMEM((3, 32, chans), BF16),
        final=pltpu.VMEM((3, parts * PIECE, LANES), F32),
        keeps=keeps,
        sends=sends,
        lands=lands,
        wsem=pltpu.SemaphoreType.DMA((11,)),
        halo_sems=pltpu.SemaphoreType.DMA((2, 2, 8)),
        core_sems=pltpu.SemaphoreType.DMA((2, parts)),
        part_sems=pltpu.SemaphoreType.DMA((parts, 3, 2, 3)),
        small_sems=pltpu.SemaphoreType.DMA((2, 7)),
    )
    rows, columns = chans // rn, hidden // (zn * xn)
    outs = pl.pallas_call(
        functools.partial(fused_kernel, mesh_sizes, scale),
        out_shape=[
            jax.ShapeDtypeStruct(feature_map.shape, BF16),
            jax.ShapeDtypeStruct(feature_map.shape, BF16),
            jax.ShapeDtypeStruct((rows, columns), F32),
            jax.ShapeDtypeStruct((rows, columns), F32),
            jax.ShapeDtypeStruct(dw_kernel.shape, F32),
            jax.ShapeDtypeStruct((5, chans), F32),
            jax.ShapeDtypeStruct((hidden,), F32),
        ],
        in_specs=[hbm] * 11,
        out_specs=[vmem] * 7,
        scratch_shapes=list(scratch.values()),
        compiler_params=pltpu.CompilerParams(
            collective_id=0, has_side_effects=True, vmem_limit_bytes=VMEM_BYTES
        ),
    )(
        feature_map,
        cotangent,
        dw_kernel,
        dw_bias,
        layer_norm_gain,
        layer_norm_bias,
        w_expand,
        b_expand,
        w_reduce,
        b_reduce,
        layer_scale,
    )
    shapes = [jax.ShapeDtypeStruct(o.shape, o.dtype) for o in outs]
    return tuple(
        pl.pallas_call(
            write_out,
            out_shape=shapes,
            in_specs=[hbm] * 7,
            out_specs=[hbm] * 7,
            scratch_shapes=[pltpu.SemaphoreType.DMA((7,))],
            compiler_params=pltpu.CompilerParams(vmem_limit_bytes=VMEM_BYTES),
        )(*outs)
    )


def write_out(*refs):
    sems = refs[14]
    copies = [pltpu.make_async_copy(refs[n], refs[7 + n], sems.at[n]) for n in range(7)]
    for copy in copies:
        copy.start()
    for copy in copies:
        copy.wait()


def fits(sizes):
    return sizes == (4, 2, 4)


def solution(mesh):
    in_specs = (
        P("rep", "rows", "cols", None),
        P(),
        P(),
        P(),
        P(),
        P(),
        P(),
        P(),
        P(),
        P(),
        P("rep", "rows", "cols", None),
    )
    out_specs = (
        P("rep", "rows", "cols", None),
        P("rep", "rows", "cols", None),
        P("rep", ("rows", "cols")),
        P("rep", ("rows", "cols")),
        P(),
        P(),
        P(),
    )
    sizes = tuple(mesh.shape[a] for a in ("rows", "cols", "rep"))
    body = functools.partial(fused, sizes) if fits(sizes) else per_device
    return jax.shard_map(
        body, mesh=mesh, in_specs=in_specs, out_specs=out_specs, check_vma=False
    )
```

```python
import functools

import jax
import jax.numpy as jnp
from jax import lax
from jax.experimental import pallas as pl
from jax.experimental.pallas import tpu as pltpu
from jax.sharding import PartitionSpec as P

MESH = pl.DeviceIdType.MESH
F32, BF16 = jnp.float32, jnp.bfloat16
LANES = 128
PIECE = 48
VMEM_BYTES = 64 * 1024 * 1024
ORDERS = ("yxz", "xyz", "zyx", "xyz", "yxz", "xyz")
DIRECTIONS = ((-1, 0), (1, 0), (0, -1), (0, 1), (-1, -1), (-1, 1), (1, -1), (1, 1))
SIZES = {"y": 2, "x": 2, "z": 4}

EPS = 1e-06
INV_ROOT_TWO = 0.7071067811865476
INV_ROOT_TWO_PI = 0.3989422804014327


def extended(cells, sides, width):
    for axis, dim in sides:
        count = lax.axis_size(axis)
        ends = count - 1
        head = lax.slice_in_dim(cells, 0, width, axis=dim)
        tail = lax.slice_in_dim(cells, cells.shape[dim] - width, cells.shape[dim], axis=dim)
        cells = jnp.concatenate(
            [
                lax.ppermute(tail, axis, [(i, (i + 1) % count) for i in range(ends)]),
                cells,
                lax.ppermute(head, axis, [((i + 1) % count, i) for i in range(ends)]),
            ],
            axis=dim,
        )
    return cells


def depthwise(padded, kernel, height, width):
    total = jnp.zeros((height, width, padded.shape[-1]), jnp.float32)
    for i in range(7):
        for j in range(7):
            total = total + kernel[i, j] * padded[i : i + height, j : j + width].astype(jnp.float32)
    return total


def front_pass(
    xpad,
    gout,
    dw_kernel,
    dw_bias,
    layer_norm_gain,
    layer_norm_bias,
    w_expand,
    b_expand,
    w_reduce,
    b_reduce,
    layer_scale,
    height,
    width,
):
    chans = xpad.shape[-1]
    conv = depthwise(xpad, dw_kernel, height, width) + dw_bias
    flat = conv.reshape(-1, chans)
    centered_input = flat - jnp.mean(flat, axis=-1, keepdims=True)
    inverse_deviation = lax.rsqrt(
        jnp.mean(centered_input * centered_input, axis=-1, keepdims=True) + EPS
    )
    standardized_input = centered_input * inverse_deviation
    normalized_rows = (standardized_input * layer_norm_gain + layer_norm_bias).astype(jnp.bfloat16)
    pre = jnp.dot(normalized_rows, w_expand, preferred_element_type=jnp.float32) + b_expand
    cdf = 0.5 * (1.0 + lax.erf(pre * INV_ROOT_TWO))
    act = (pre * cdf).astype(jnp.bfloat16)
    branch = jnp.dot(act, w_reduce, preferred_element_type=jnp.float32) + b_reduce
    inner = xpad[3 : 3 + height, 3 : 3 + width].reshape(-1, chans).astype(jnp.float32)
    block_out = (inner + layer_scale * branch).astype(jnp.bfloat16).reshape(height, width, chans)
    grad = gout.reshape(-1, chans).astype(jnp.float32)
    scaled = grad * layer_scale
    g_branch = scaled.astype(jnp.bfloat16)
    g_scale = jnp.sum(grad * branch, axis=0)
    g_breduce = jnp.sum(scaled, axis=0)
    grad_reduce_t = lax.dot_general(
        g_branch, act, (((0,), (0,)), ((), ())), preferred_element_type=jnp.float32
    )
    g_act = lax.dot_general(
        g_branch, w_reduce, (((1,), (1,)), ((), ())), preferred_element_type=jnp.float32
    )
    pdf = jnp.exp(-0.5 * pre * pre) * INV_ROOT_TWO_PI
    g_pre = g_act * (cdf + pre * pdf)
    g_bexp = jnp.sum(g_pre, axis=0)
    g_pre_b = g_pre.astype(jnp.bfloat16)
    grad_expand = lax.dot_general(
        normalized_rows, g_pre_b, (((0,), (0,)), ((), ())), preferred_element_type=jnp.float32
    )
    grad_normalized = lax.dot_general(
        g_pre_b, w_expand, (((1,), (1,)), ((), ())), preferred_element_type=jnp.float32
    )
    grad_norm_gain = jnp.sum(grad_normalized * standardized_input, axis=0)
    g_lnbias = jnp.sum(grad_normalized, axis=0)
    scaled_grad_input = grad_normalized * layer_norm_gain
    grad_convolution = inverse_deviation * (
        scaled_grad_input
        - jnp.mean(scaled_grad_input, axis=-1, keepdims=True)
        - standardized_input
        * jnp.mean(scaled_grad_input * standardized_input, axis=-1, keepdims=True)
    )
    g_dwbias = jnp.sum(grad_convolution, axis=0)
    vectors = jnp.stack([g_dwbias, grad_norm_gain, g_lnbias, g_breduce, g_scale])
    return (
        block_out,
        grad_convolution.reshape(height, width, chans),
        grad_expand,
        grad_reduce_t,
        vectors,
        g_bexp,
    )


def back_pass(gpad, xpad, gout, dw_kernel, height, width):
    inner = gpad[3 : 3 + height, 3 : 3 + width]
    grad_in = gout.astype(jnp.float32)
    kernel_rows = []
    for i in range(7):
        row_terms = []
        for j in range(7):
            part = xpad[i : i + height, j : j + width].astype(jnp.float32)
            row_terms.append(jnp.sum(inner * part, axis=(0, 1)))
            grad_in = (
                grad_in + dw_kernel[i, j] * gpad[6 - i : 6 - i + height, 6 - j : 6 - j + width]
            )
        kernel_rows.append(jnp.stack(row_terms))
    return (grad_in.astype(jnp.bfloat16), jnp.stack(kernel_rows))


def per_device(
    feature_map,
    dw_kernel,
    dw_bias,
    layer_norm_gain,
    layer_norm_bias,
    w_expand,
    b_expand,
    w_reduce,
    b_reduce,
    layer_scale,
    cotangent,
):
    height, width = (feature_map.shape[1], feature_map.shape[2])
    xpad = extended(feature_map, (("rows", 1), ("cols", 2)), 3)[0]
    gout = cotangent[0]
    block_out, grad_convolution, gexp, gred, vectors, gbexp = front_pass(
        xpad,
        gout,
        dw_kernel,
        dw_bias,
        layer_norm_gain,
        layer_norm_bias,
        w_expand,
        b_expand,
        w_reduce,
        b_reduce,
        layer_scale,
        height,
        width,
    )
    stacked = jnp.stack([gexp, gred])
    gpad = extended(grad_convolution, (("rows", 0), ("cols", 1)), 3)
    grad_in, gker = back_pass(gpad, xpad, gout, dw_kernel, height, width)
    partial_sum = lax.psum_scatter(stacked, "rep", scatter_dimension=1, tiled=True)
    summed = lax.psum_scatter(partial_sum, ("rows", "cols"), scatter_dimension=2, tiled=True)
    gker, vectors, gbexp = lax.psum((gker, vectors, gbexp), ("rows", "cols", "rep"))
    count = lax.axis_size("rows") * height * lax.axis_size("cols") * width * lax.axis_size("rep")
    scale = 1.0 / jnp.sqrt(jnp.float32(count))
    return (
        block_out[None],
        grad_in[None],
        summed[0] * scale,
        summed[1] * scale,
        gker * scale,
        vectors * scale,
        gbexp * scale,
    )


def pack_rows(value):
    half = value.shape[0] // 2
    return jnp.concatenate([value[:half, :8], value[half:, :8]], axis=1)


def halo_source(cells, dz, dx):
    rows = cells
    if dz == -1:
        rows = cells[:4] if dx else cells[:3]
    elif dz == 1:
        rows = cells[4:] if dx else cells[5:]
    if dx == 0:
        return rows.astype(BF16)
    return pack_rows(rows[:, :8] if dx == -1 else rows[:, 8:]).astype(BF16)


def halo_target(padded, landed, dz, dx):
    if dx:
        half = landed.shape[0]
        landed = jnp.concatenate([landed[:, :8], landed[:, 8:]], axis=0)
        if dz == 1:
            landed = landed[1:]
        elif dz == -1:
            landed = landed[:3]
    rows = slice(3, 11) if dz == 0 else (slice(0, 3) if dz == 1 else slice(11, 14))
    columns = slice(8, 24) if dx == 0 else (slice(0, 8) if dx == 1 else slice(24, 32))
    padded[rows, columns, :] = landed


def halo_shape(dz, dx, chans):
    if dx == 0:
        return (3, 16, chans)
    return (4 if dz == 0 else 2, 16, chans)


def fused_kernel(
    sizes,
    scale,
    x_hbm,
    gout_hbm,
    dwk_hbm,
    dwb_hbm,
    gain_hbm,
    lnb_hbm,
    wexp_hbm,
    bexp_hbm,
    wred_hbm,
    bred_hbm,
    ls_hbm,
    out_ref,
    gin_ref,
    gexp_ref,
    gred_ref,
    gker_ref,
    gvec_ref,
    gbexp_ref,
    x_ref,
    gout_ref,
    dwk_ref,
    dwb_1d,
    gain_1d,
    lnb_1d,
    wexp,
    bexp_1d,
    wred,
    bred_1d,
    ls_1d,
    bexp_ref,
    pre_s,
    gact_s,
    xp,
    gp,
    work,
    xhat_s,
    lhs_t,
    act_s,
    gpre_s,
    main0,
    main1,
    rem,
    grad_out_blocks,
    landed0,
    xsend,
    xland,
    gsend,
    gland,
    small,
    small_send,
    small_land,
    zsend,
    zland,
    final,
    keeps,
    sends,
    lands,
    wsem,
    halo_sems,
    core_sems,
    part_sems,
    small_sems,
):
    zn, xn, rn = sizes
    z, x, r = lax.axis_index("rows"), lax.axis_index("cols"), lax.axis_index("rep")
    y, c = r // 2, r % 2
    chans = x_ref.shape[-1]
    hidden = wexp.shape[1]
    core_mate = {"rows": z, "cols": x, "rep": 2 * y + 1 - c}
    y_mate = {"rows": z, "cols": x, "rep": 2 * (1 - y) + c}
    x_mate = {"rows": z, "cols": 1 - x, "rep": r}

    def z_mate(d):
        return {"rows": (z + d) % zn, "cols": x, "rep": r}

    fetches = [
        pltpu.make_async_copy(source, target, wsem.at[n])
        for n, (source, target) in enumerate(
            (
                (x_hbm, x_ref),
                (gout_hbm, gout_ref),
                (ls_hbm, ls_1d),
                (wred_hbm, wred),
                (dwb_hbm, dwb_1d),
                (dwk_hbm, dwk_ref),
                (gain_hbm, gain_1d),
                (lnb_hbm, lnb_1d),
                (bexp_hbm, bexp_1d),
                (bred_hbm, bred_1d),
                (wexp_hbm, wexp),
            )
        )
    ]
    for copy in fetches:
        copy.start()

    def inside(a, b):
        return (a >= 0) & (a < zn) & (b >= 0) & (b < xn)

    barrier = pltpu.get_barrier_semaphore()
    greeted = jnp.int32(6)
    for mate in [core_mate, y_mate, x_mate] + [z_mate(d) for d in (1, 2, 3)]:
        pl.semaphore_signal(barrier, inc=1, device_id=mate, device_id_type=MESH)
    for dz, dx in DIRECTIONS:
        if dx == 0 or dz == 0:
            continue
        near = inside(z + dz, x + dx)

        @pl.when(near)
        def _():
            pl.semaphore_signal(
                barrier,
                inc=1,
                device_id={"rows": z + dz, "cols": x + dx, "rep": r},
                device_id_type=MESH,
            )

        greeted = greeted + near.astype(jnp.int32)

    xp[...] = jnp.zeros_like(xp)
    gp[...] = jnp.zeros_like(gp)
    small[...] = jnp.zeros_like(small)
    fetches[0].wait()
    cells = x_ref[0].astype(F32)
    for n, (dz, dx) in enumerate(DIRECTIONS):
        xsend[n][...] = halo_source(cells, dz, dx)
    xp[3:11, 8:24, :] = cells
    pl.semaphore_wait(barrier, greeted)

    def halo_copy(which, n):
        source, target = ((xsend, xland), (gsend, gland))[which]
        dz, dx = DIRECTIONS[n]
        return pltpu.make_async_remote_copy(
            src_ref=source[n],
            dst_ref=target[n],
            send_sem=halo_sems.at[which, 0, n],
            recv_sem=halo_sems.at[which, 1, n],
            device_id={"rows": z + dz, "cols": x + dx, "rep": r},
            device_id_type=MESH,
        )

    def halo_start(which):
        for n, (dz, dx) in enumerate(DIRECTIONS):
            pl.when(inside(z + dz, x + dx))(lambda n=n: halo_copy(which, n).start())

    def halo_finish(which, padded):
        landed = (xland, gland)[which]
        for n, (dz, dx) in enumerate(DIRECTIONS):

            @pl.when(inside(z - dz, x - dx))
            def _(n=n, dz=dz, dx=dx):
                halo_copy(which, n).wait_recv()
                halo_target(padded, landed[n][...].astype(F32), dz, dx)

    def halo_sent(which):
        for n, (dz, dx) in enumerate(DIRECTIONS):
            pl.when(inside(z + dz, x + dx))(lambda n=n: halo_copy(which, n).wait_send())

    halo_start(0)
    for copy in fetches[1:10]:
        copy.wait()

    def row(ref):
        return ref[...].reshape(1, -1)

    layer_scale, gain = row(ls_1d), row(gain_1d)
    bexp_ref[...] = row(bexp_1d)
    grad = gout_ref[0].astype(F32).reshape(-1, chans)
    scaled = grad * layer_scale
    g_branch = scaled.astype(BF16)
    small[52:53, :] = jnp.sum(scaled, axis=0, keepdims=True)
    contract_last = (((1,), (1,)), ((), ()))
    gact_s[...] = lax.dot_general(g_branch, wred[...], contract_last, preferred_element_type=F32)
    lhs_t[1] = scaled.T.astype(BF16).reshape(rn, chans // rn, 128)
    bias = row(dwb_1d)
    work[...] = jnp.broadcast_to(bias, work.shape)
    halo_finish(0, xp)

    def conv_chunk(n, carry):
        ch = pl.ds(pl.multiple_of(n * LANES, LANES), LANES)
        total = work[:, ch].reshape(8, 16, LANES)
        for j in range(7):
            shifted = xp[:, 5 + j : 21 + j, ch]
            for i in range(7):
                total = total + dwk_ref[i, j : j + 1, ch] * shifted[i : i + 8]
        work[:, ch] = total.reshape(128, LANES)
        return carry

    lax.fori_loop(0, chans // LANES, conv_chunk, 0)
    conv = work[...]
    centered = conv - jnp.mean(conv, axis=-1, keepdims=True)
    rstd = lax.rsqrt(jnp.mean(centered * centered, axis=-1, keepdims=True) + EPS)
    xhat = centered * rstd
    xhat_s[...] = xhat
    normed32 = xhat * gain + row(lnb_1d)
    normed = normed32.astype(BF16)
    lhs_t[0] = normed32.T.astype(BF16).reshape(rn, chans // rn, 128)
    fetches[10].wait()
    pre_s[...] = jnp.dot(normed, wexp[...], preferred_element_type=F32)

    lower = lax.broadcasted_iota(jnp.int32, (64, LANES), 1) < LANES // 2
    zero = jnp.zeros((64, LANES), F32)

    def hidden_pair(n, carry):
        here = pl.multiple_of(n * 3 * LANES, LANES)
        even = pl.ds(pl.multiple_of(2 * n * LANES, LANES), LANES)
        odd = pl.ds(pl.multiple_of(2 * n * LANES + LANES, LANES), LANES)
        sums = []
        for group in range(3):
            ch = pl.ds(pl.multiple_of(here + group * LANES, LANES), LANES)
            sums.append(jnp.zeros((1, LANES), F32))
            for top in (0, 64):
                rows = slice(top, top + 64)
                after = slice(128 + top, 192 + top)
                pre = pre_s[rows, ch] + bexp_ref[:, ch]
                cdf = 0.5 * (1.0 + lax.erf(pre * INV_ROOT_TWO))
                act = pre * cdf
                pdf = jnp.exp(-0.5 * pre * pre) * INV_ROOT_TWO_PI
                g_pre = gact_s[rows, ch] * (cdf + pre * pdf)
                sums[-1] = sums[-1] + jnp.sum(g_pre, axis=0, keepdims=True)
                act_s[rows, ch] = act.astype(BF16)
                gpre_s[rows, ch] = g_pre.astype(BF16)
                if group == 1:
                    rolled = pltpu.roll(act, LANES // 2, 1)
                    rem[rows, even] = jnp.where(lower, g_pre, zero).astype(BF16)
                    rem[after, even] = jnp.where(lower, zero, rolled).astype(BF16)
                    rem[rows, odd] = jnp.where(lower, zero, g_pre).astype(BF16)
                    rem[after, odd] = jnp.where(lower, rolled, zero).astype(BF16)
                else:
                    to = odd if group else even
                    main0[rows, to] = g_pre.astype(BF16)
                    main1[rows, to] = act.astype(BF16)
        bexp_ref[:, pl.ds(here, 3 * LANES)] = jnp.concatenate(sums, axis=1)
        return carry

    lax.fori_loop(0, zn, hidden_pair, 0)
    for n in range(hidden // chans):
        small[54 + n : 55 + n, :] = bexp_ref[:, n * chans : (n + 1) * chans]

    def left_of(owner):
        left0 = jnp.concatenate([lhs_t[0, owner], lhs_t[0, 2 + owner]], axis=0)
        left1 = jnp.concatenate([lhs_t[1, owner], lhs_t[1, 2 + owner]], axis=0)
        return left0, left1, jnp.concatenate([left0, left1], axis=1)

    def products(owner, lefts, k):
        right = (main0, main1, rem)[k]
        for zz in range(zn):
            block = jnp.dot(
                lefts[k], right[:, 2 * zz * LANES : (2 * zz + 2) * LANES], preferred_element_type=F32
            ).astype(BF16)
            for xx in range(xn):
                for yy in range(2):
                    for h in range(2):
                        at = (2 * yy + h) * PIECE
                        grad_out_blocks[owner, 2 * k + h, yy, xx, zz] = block[
                            at : at + PIECE, xx * LANES : (xx + 1) * LANES
                        ]

    def core_copy(p):
        return pltpu.make_async_remote_copy(
            src_ref=grad_out_blocks.at[1 - c, p],
            dst_ref=landed0.at[p],
            send_sem=core_sems.at[0, p],
            recv_sem=core_sems.at[1, p],
            device_id=core_mate,
            device_id_type=MESH,
        )

    parts = len(ORDERS)
    lefts = left_of(1 - c)
    for k in range(3):
        products(1 - c, lefts, k)
        core_copy(2 * k).start()
        core_copy(2 * k + 1).start()

    def place(dims, axis, index):
        return tuple(index if d == axis else slice(None) for d in dims)

    def stage_copies(p, s):
        axis = ORDERS[p][s]
        if axis == "z":
            return [
                pltpu.make_async_remote_copy(
                    src_ref=sends[p][s].at[d - 1],
                    dst_ref=lands[p][s].at[d - 1],
                    send_sem=part_sems.at[p, s, 0, d - 1],
                    recv_sem=part_sems.at[p, s, 1, d - 1],
                    device_id=z_mate(d),
                    device_id_type=MESH,
                )
                for d in (1, 2, 3)
            ]
        return [
            pltpu.make_async_remote_copy(
                src_ref=sends[p][s].at[0],
                dst_ref=lands[p][s].at[0],
                send_sem=part_sems.at[p, s, 0, 0],
                recv_sem=part_sems.at[p, s, 1, 0],
                device_id=y_mate if axis == "y" else x_mate,
                device_id_type=MESH,
            )
        ]

    def load(p, s, at):
        if s == 0:
            return grad_out_blocks[(c, p) + at].astype(F32) + landed0[(p,) + at].astype(F32)
        total = keeps[p][s - 1][at]
        for d in range(lands[p][s - 1].shape[0]):
            total = total + lands[p][s - 1][(d,) + at].astype(F32)
        return total

    def stage(p, s):
        if s == 0:
            core_copy(p).wait_recv()
        else:
            for copy in stage_copies(p, s - 1):
                copy.wait_recv()
        dims = [d for d in "yxz" if d not in ORDERS[p][:s]]
        if s == 3:
            final[p // 2, (p % 2) * PIECE : (p % 2 + 1) * PIECE, :] = load(p, s, ())
            return
        axis = ORDERS[p][s]
        copies = stage_copies(p, s)
        if axis == "z":
            for d in (1, 2, 3):
                sends[p][s][d - 1] = load(p, s, place(dims, "z", (z + d) % zn)).astype(BF16)
                copies[d - 1].start()
            keeps[p][s][...] = load(p, s, place(dims, "z", z))
        else:
            mine = y if axis == "y" else x
            sends[p][s][0] = load(p, s, place(dims, axis, 1 - mine)).astype(BF16)
            copies[0].start()
            keeps[p][s][...] = load(p, s, place(dims, axis, mine))

    lefts = left_of(c)
    for k in range(3):
        products(c, lefts, k)
        stage(2 * k, 0)
        stage(2 * k + 1, 0)

    g_normed = lax.dot_general(gpre_s[...], wexp[...], contract_last, preferred_element_type=F32)
    xhat = xhat_s[...]
    small[50:51, :] = jnp.sum(g_normed * xhat, axis=0, keepdims=True)
    small[51:52, :] = jnp.sum(g_normed, axis=0, keepdims=True)
    gx = g_normed * gain
    g_conv = rstd * (
        gx
        - jnp.mean(gx, axis=-1, keepdims=True)
        - xhat * jnp.mean(gx * xhat, axis=-1, keepdims=True)
    )
    small[49:50, :] = jnp.sum(g_conv, axis=0, keepdims=True)
    g_cells = g_conv.reshape(8, 16, chans)
    for n, (dz, dx) in enumerate(DIRECTIONS):
        gsend[n][...] = halo_source(g_cells, dz, dx)
    halo_start(1)
    gp[3:11, 8:24, :] = g_cells

    branch = jnp.dot(act_s[...], wred[...], preferred_element_type=F32) + row(bred_1d)
    small[53:54, :] = jnp.sum(grad * branch, axis=0, keepdims=True)
    inner = x_ref[0].astype(F32).reshape(-1, chans)
    out_ref[0] = (inner + layer_scale * branch).astype(BF16).reshape(8, 16, chans)

    for p in range(3):
        stage(p, 1)

    def kernel_chunk(n, carry):
        ch = pl.ds(pl.multiple_of(n * LANES, LANES), LANES)
        own = gp[3:11, 8:24, ch]
        for j in range(7):
            shifted = xp[:, 5 + j : 21 + j, ch]
            for i in range(7):
                terms = jnp.sum((own * shifted[i : i + 8]).reshape(16, 8, LANES), axis=0)
                small[7 * i + j : 7 * i + j + 1, ch] = jnp.sum(terms, axis=0, keepdims=True)
        return carry

    lax.fori_loop(0, chans // LANES, kernel_chunk, 0)

    half = small.shape[0] // 2

    def small_copy(n, source, target, mate):
        return pltpu.make_async_remote_copy(
            src_ref=source,
            dst_ref=target,
            send_sem=small_sems.at[0, n],
            recv_sem=small_sems.at[1, n],
            device_id=mate,
            device_id_type=MESH,
        )

    moves = [small_copy(n, small_send.at[n], small_land.at[n], m) for n, m in enumerate((core_mate, y_mate, x_mate))]
    z_moves = [small_copy(2 + d, zsend, zland.at[d - 1], z_mate(d)) for d in (1, 2, 3)]
    other_rows = pl.ds(pl.multiple_of((1 - c) * half, half), half)
    my_rows = pl.ds(pl.multiple_of(c * half, half), half)
    small_send[0] = small[other_rows, :]
    moves[0].start()

    for p in range(3, parts):
        stage(p, 1)

    moves[0].wait_recv()
    small_send[1] = small[my_rows, :] + small_land[0]
    moves[1].start()
    for p in range(3):
        stage(p, 2)
    moves[1].wait_recv()
    small_send[2] = small_send[1] + small_land[1]
    moves[2].start()
    for p in range(3, parts):
        stage(p, 2)
    moves[2].wait_recv()
    zsend[...] = (small_send[2] + small_land[2]).astype(BF16)
    for move in z_moves:
        move.start()

    halo_finish(1, gp)

    def input_chunk(n, carry):
        ch = pl.ds(pl.multiple_of(n * LANES, LANES), LANES)
        total = gout_ref[0, :, :, ch].astype(F32)
        for j in range(7):
            shifted = gp[:, 11 - j : 27 - j, ch]
            for i in range(7):
                total = total + dwk_ref[i, j : j + 1, ch] * shifted[6 - i : 14 - i]
        gin_ref[0, :, :, ch] = total.astype(BF16)
        return carry

    lax.fori_loop(0, chans // LANES, input_chunk, 0)

    for move in z_moves:
        move.wait_recv()
    quarter = [zsend[...].astype(F32)] + [zland[d].astype(F32) for d in range(3)]
    total = jnp.zeros_like(quarter[0])
    for at in range(zn):
        d = (z - at) % zn
        term = quarter[0]
        for k in (1, 2, 3):
            term = jnp.where(d == k, quarter[k], term)
        total = total + term
    small_send[3] = total * scale
    last = small_copy(6, small_send.at[3], small_land.at[3], core_mate)
    last.start()

    for p in range(parts):
        stage(p, 3)
    blocks = final[...] * scale
    wide = LANES + LANES // 2
    m0, m1, mixed = blocks[0], blocks[1], blocks[2]
    first, second = mixed[:, : LANES // 2], mixed[:, LANES // 2 :]

    @pl.when(x == 0)
    def _():
        gexp_ref[:, :LANES] = m0
        gexp_ref[:, LANES:wide] = first
        gred_ref[:, :LANES] = m1
        gred_ref[:, LANES:wide] = second

    @pl.when(x == 1)
    def _():
        gexp_ref[...] = jnp.concatenate([second, m0], axis=1)
        gred_ref[...] = jnp.concatenate([first, m1], axis=1)

    last.wait_recv()
    small[my_rows, :] = small_send[3]
    small[other_rows, :] = small_land[3]
    for i in range(7):
        gker_ref[i] = small[7 * i : 7 * i + 7, :]
    gvec_ref[...] = small[49:54, :]
    for n in range(hidden // chans):
        bexp_ref[:, n * chans : (n + 1) * chans] = small[54 + n : 55 + n, :]
    gbexp_ref[...] = bexp_ref[...].reshape(-1)

    halo_sent(0)
    halo_sent(1)
    for p in range(parts):
        core_copy(p).wait_send()
        for s in range(3):
            for copy in stage_copies(p, s):
                copy.wait_send()
    for move in moves + z_moves + [last]:
        move.wait_send()


def fused(mesh_sizes, *args):
    (
        feature_map,
        dw_kernel,
        dw_bias,
        layer_norm_gain,
        layer_norm_bias,
        w_expand,
        b_expand,
        w_reduce,
        b_reduce,
        layer_scale,
        cotangent,
    ) = args
    zn, xn, rn = mesh_sizes
    _, height, width, chans = feature_map.shape
    hidden = w_expand.shape[1]
    pixels = height * width * zn * xn * rn
    scale = float(pixels) ** -0.5
    vmem = pl.BlockSpec(memory_space=pltpu.VMEM)
    hbm = pl.BlockSpec(memory_space=pltpu.HBM)
    parts = len(ORDERS)
    block = (PIECE, LANES)
    keeps, sends, lands = [], [], []
    for order in ORDERS:
        keeps.append([])
        sends.append([])
        lands.append([])
        for s in range(3):
            left = tuple(SIZES[d] for d in "yxz" if d not in order[: s + 1])
            copies = 3 if order[s] == "z" else 1
            keeps[-1].append(pltpu.VMEM(left + block, F32))
            sends[-1].append(pltpu.VMEM((copies,) + left + block, BF16))
            lands[-1].append(pltpu.VMEM((copies,) + left + block, BF16))
    halos = [pltpu.VMEM(halo_shape(dz, dx, chans), BF16) for dz, dx in DIRECTIONS]
    scratch = dict(
        x_ref=pltpu.VMEM(feature_map.shape, BF16),
        gout_ref=pltpu.VMEM(cotangent.shape, BF16),
        dwk_ref=pltpu.VMEM(dw_kernel.shape, F32),
        dwb_1d=pltpu.VMEM((chans,), F32),
        gain_1d=pltpu.VMEM((chans,), F32),
        lnb_1d=pltpu.VMEM((chans,), F32),
        wexp=pltpu.VMEM(w_expand.shape, BF16),
        bexp_1d=pltpu.VMEM((hidden,), F32),
        wred=pltpu.VMEM(w_reduce.shape, BF16),
        bred_1d=pltpu.VMEM((chans,), F32),
        ls_1d=pltpu.VMEM((chans,), F32),
        bexp_ref=pltpu.VMEM((1, hidden), F32),
        pre_s=pltpu.VMEM((128, hidden), F32),
        gact_s=pltpu.VMEM((128, hidden), F32),
        xp=pltpu.VMEM((14, 32, chans), F32),
        gp=pltpu.VMEM((14, 32, chans), F32),
        work=pltpu.VMEM((128, chans), F32),
        xhat_s=pltpu.VMEM((128, chans), F32),
        lhs_t=pltpu.VMEM((2, rn, chans // rn, 128), BF16),
        act_s=pltpu.VMEM((128, hidden), BF16),
        gpre_s=pltpu.VMEM((128, hidden), BF16),
        main0=pltpu.VMEM((128, 2 * zn * LANES), BF16),
        main1=pltpu.VMEM((128, 2 * zn * LANES), BF16),
        rem=pltpu.VMEM((256, 2 * zn * LANES), BF16),
        grad_out_blocks=pltpu.VMEM((2, parts, 2, xn, zn) + block, BF16),
        landed0=pltpu.VMEM((parts, 2, xn, zn) + block, BF16),
        xsend=list(halos),
        xland=list(halos),
        gsend=list(halos),
        gland=list(halos),
        small=pltpu.VMEM((64, chans), F32),
        small_send=pltpu.VMEM((4, 32, chans), F32),
        small_land=pltpu.VMEM((4, 32, chans), F32),
        zsend=pltpu.VMEM((32, chans), BF16),
        zland=pltpu.VMEM((3, 32, chans), BF16),
        final=pltpu.VMEM((3, 2 * PIECE, LANES), F32),
        keeps=keeps,
        sends=sends,
        lands=lands,
        wsem=pltpu.SemaphoreType.DMA((11,)),
        halo_sems=pltpu.SemaphoreType.DMA((2, 2, 8)),
        core_sems=pltpu.SemaphoreType.DMA((2, parts)),
        part_sems=pltpu.SemaphoreType.DMA((parts, 3, 2, 3)),
        small_sems=pltpu.SemaphoreType.DMA((2, 7)),
    )
    rows, columns = chans // rn, hidden // (zn * xn)
    outs = pl.pallas_call(
        functools.partial(fused_kernel, mesh_sizes, scale),
        out_shape=[
            jax.ShapeDtypeStruct(feature_map.shape, BF16),
            jax.ShapeDtypeStruct(feature_map.shape, BF16),
            jax.ShapeDtypeStruct((rows, columns), F32),
            jax.ShapeDtypeStruct((rows, columns), F32),
            jax.ShapeDtypeStruct(dw_kernel.shape, F32),
            jax.ShapeDtypeStruct((5, chans), F32),
            jax.ShapeDtypeStruct((hidden,), F32),
        ],
        in_specs=[hbm] * 11,
        out_specs=[vmem] * 7,
        scratch_shapes=list(scratch.values()),
        compiler_params=pltpu.CompilerParams(
            collective_id=0, has_side_effects=True, vmem_limit_bytes=VMEM_BYTES
        ),
    )(
        feature_map,
        cotangent,
        dw_kernel,
        dw_bias,
        layer_norm_gain,
        layer_norm_bias,
        w_expand,
        b_expand,
        w_reduce,
        b_reduce,
        layer_scale,
    )
    shapes = [jax.ShapeDtypeStruct(o.shape, o.dtype) for o in outs]
    return tuple(
        pl.pallas_call(
            write_out,
            out_shape=shapes,
            in_specs=[hbm] * 7,
            out_specs=[hbm] * 7,
            scratch_shapes=[pltpu.VMEM(o.shape, o.dtype) for o in outs]
            + [pltpu.SemaphoreType.DMA((2, 7))],
            compiler_params=pltpu.CompilerParams(vmem_limit_bytes=VMEM_BYTES),
        )(*outs)
    )


def write_out(*refs):
    sems = refs[21]
    reads = [pltpu.make_async_copy(refs[n], refs[14 + n], sems.at[0, n]) for n in range(7)]
    writes = [pltpu.make_async_copy(refs[14 + n], refs[7 + n], sems.at[1, n]) for n in range(7)]
    for copy in reads:
        copy.start()
    for read, write in zip(reads, writes):
        read.wait()
        write.start()
    for copy in writes:
        copy.wait()


def fits(sizes):
    return sizes == (4, 2, 4)


def solution(mesh):
    in_specs = (
        P("rep", "rows", "cols", None),
        P(),
        P(),
        P(),
        P(),
        P(),
        P(),
        P(),
        P(),
        P(),
        P("rep", "rows", "cols", None),
    )
    out_specs = (
        P("rep", "rows", "cols", None),
        P("rep", "rows", "cols", None),
        P("rep", ("rows", "cols")),
        P("rep", ("rows", "cols")),
        P(),
        P(),
        P(),
    )
    sizes = tuple(mesh.shape[a] for a in ("rows", "cols", "rep"))
    body = functools.partial(fused, sizes) if fits(sizes) else per_device
    return jax.shard_map(
        body, mesh=mesh, in_specs=in_specs, out_specs=out_specs, check_vma=False
    )
```

```python
import functools

import jax
import jax.numpy as jnp
from jax import lax
from jax.experimental import pallas as pl
from jax.experimental.pallas import tpu as pltpu
from jax.sharding import PartitionSpec as P

MESH = pl.DeviceIdType.MESH
F32, BF16 = jnp.float32, jnp.bfloat16
LANES = 128
PIECE = 48
VMEM_BYTES = 64 * 1024 * 1024
ORDERS = ("yxz", "xyz", "zyx", "xyz", "yxz", "xyz")
DIRECTIONS = ((-1, 0), (1, 0), (0, -1), (0, 1), (-1, -1), (-1, 1), (1, -1), (1, 1))
SIZES = {"y": 2, "x": 2, "z": 4}

EPS = 1e-06
INV_ROOT_TWO = 0.7071067811865476
INV_ROOT_TWO_PI = 0.3989422804014327


def extended(cells, sides, width):
    for axis, dim in sides:
        count = lax.axis_size(axis)
        ends = count - 1
        head = lax.slice_in_dim(cells, 0, width, axis=dim)
        tail = lax.slice_in_dim(cells, cells.shape[dim] - width, cells.shape[dim], axis=dim)
        cells = jnp.concatenate(
            [
                lax.ppermute(tail, axis, [(i, (i + 1) % count) for i in range(ends)]),
                cells,
                lax.ppermute(head, axis, [((i + 1) % count, i) for i in range(ends)]),
            ],
            axis=dim,
        )
    return cells


def depthwise(padded, kernel, height, width):
    total = jnp.zeros((height, width, padded.shape[-1]), jnp.float32)
    for i in range(7):
        for j in range(7):
            total = total + kernel[i, j] * padded[i : i + height, j : j + width].astype(jnp.float32)
    return total


def front_pass(
    xpad,
    gout,
    dw_kernel,
    dw_bias,
    layer_norm_gain,
    layer_norm_bias,
    w_expand,
    b_expand,
    w_reduce,
    b_reduce,
    layer_scale,
    height,
    width,
):
    chans = xpad.shape[-1]
    conv = depthwise(xpad, dw_kernel, height, width) + dw_bias
    flat = conv.reshape(-1, chans)
    centered_input = flat - jnp.mean(flat, axis=-1, keepdims=True)
    inverse_deviation = lax.rsqrt(
        jnp.mean(centered_input * centered_input, axis=-1, keepdims=True) + EPS
    )
    standardized_input = centered_input * inverse_deviation
    normalized_rows = (standardized_input * layer_norm_gain + layer_norm_bias).astype(jnp.bfloat16)
    pre = jnp.dot(normalized_rows, w_expand, preferred_element_type=jnp.float32) + b_expand
    cdf = 0.5 * (1.0 + lax.erf(pre * INV_ROOT_TWO))
    act = (pre * cdf).astype(jnp.bfloat16)
    branch = jnp.dot(act, w_reduce, preferred_element_type=jnp.float32) + b_reduce
    inner = xpad[3 : 3 + height, 3 : 3 + width].reshape(-1, chans).astype(jnp.float32)
    block_out = (inner + layer_scale * branch).astype(jnp.bfloat16).reshape(height, width, chans)
    grad = gout.reshape(-1, chans).astype(jnp.float32)
    scaled = grad * layer_scale
    g_branch = scaled.astype(jnp.bfloat16)
    g_scale = jnp.sum(grad * branch, axis=0)
    g_breduce = jnp.sum(scaled, axis=0)
    grad_reduce_t = lax.dot_general(
        g_branch, act, (((0,), (0,)), ((), ())), preferred_element_type=jnp.float32
    )
    g_act = lax.dot_general(
        g_branch, w_reduce, (((1,), (1,)), ((), ())), preferred_element_type=jnp.float32
    )
    pdf = jnp.exp(-0.5 * pre * pre) * INV_ROOT_TWO_PI
    g_pre = g_act * (cdf + pre * pdf)
    g_bexp = jnp.sum(g_pre, axis=0)
    g_pre_b = g_pre.astype(jnp.bfloat16)
    grad_expand = lax.dot_general(
        normalized_rows, g_pre_b, (((0,), (0,)), ((), ())), preferred_element_type=jnp.float32
    )
    grad_normalized = lax.dot_general(
        g_pre_b, w_expand, (((1,), (1,)), ((), ())), preferred_element_type=jnp.float32
    )
    grad_norm_gain = jnp.sum(grad_normalized * standardized_input, axis=0)
    g_lnbias = jnp.sum(grad_normalized, axis=0)
    scaled_grad_input = grad_normalized * layer_norm_gain
    grad_convolution = inverse_deviation * (
        scaled_grad_input
        - jnp.mean(scaled_grad_input, axis=-1, keepdims=True)
        - standardized_input
        * jnp.mean(scaled_grad_input * standardized_input, axis=-1, keepdims=True)
    )
    g_dwbias = jnp.sum(grad_convolution, axis=0)
    vectors = jnp.stack([g_dwbias, grad_norm_gain, g_lnbias, g_breduce, g_scale])
    return (
        block_out,
        grad_convolution.reshape(height, width, chans),
        grad_expand,
        grad_reduce_t,
        vectors,
        g_bexp,
    )


def back_pass(gpad, xpad, gout, dw_kernel, height, width):
    inner = gpad[3 : 3 + height, 3 : 3 + width]
    grad_in = gout.astype(jnp.float32)
    kernel_rows = []
    for i in range(7):
        row_terms = []
        for j in range(7):
            part = xpad[i : i + height, j : j + width].astype(jnp.float32)
            row_terms.append(jnp.sum(inner * part, axis=(0, 1)))
            grad_in = (
                grad_in + dw_kernel[i, j] * gpad[6 - i : 6 - i + height, 6 - j : 6 - j + width]
            )
        kernel_rows.append(jnp.stack(row_terms))
    return (grad_in.astype(jnp.bfloat16), jnp.stack(kernel_rows))


def per_device(
    feature_map,
    dw_kernel,
    dw_bias,
    layer_norm_gain,
    layer_norm_bias,
    w_expand,
    b_expand,
    w_reduce,
    b_reduce,
    layer_scale,
    cotangent,
):
    height, width = (feature_map.shape[1], feature_map.shape[2])
    xpad = extended(feature_map, (("rows", 1), ("cols", 2)), 3)[0]
    gout = cotangent[0]
    block_out, grad_convolution, gexp, gred, vectors, gbexp = front_pass(
        xpad,
        gout,
        dw_kernel,
        dw_bias,
        layer_norm_gain,
        layer_norm_bias,
        w_expand,
        b_expand,
        w_reduce,
        b_reduce,
        layer_scale,
        height,
        width,
    )
    stacked = jnp.stack([gexp, gred])
    gpad = extended(grad_convolution, (("rows", 0), ("cols", 1)), 3)
    grad_in, gker = back_pass(gpad, xpad, gout, dw_kernel, height, width)
    partial_sum = lax.psum_scatter(stacked, "rep", scatter_dimension=1, tiled=True)
    summed = lax.psum_scatter(partial_sum, ("rows", "cols"), scatter_dimension=2, tiled=True)
    gker, vectors, gbexp = lax.psum((gker, vectors, gbexp), ("rows", "cols", "rep"))
    count = lax.axis_size("rows") * height * lax.axis_size("cols") * width * lax.axis_size("rep")
    scale = 1.0 / jnp.sqrt(jnp.float32(count))
    return (
        block_out[None],
        grad_in[None],
        summed[0] * scale,
        summed[1] * scale,
        gker * scale,
        vectors * scale,
        gbexp * scale,
    )


def pack_rows(value):
    half = value.shape[0] // 2
    return jnp.concatenate([value[:half, :8], value[half:, :8]], axis=1)


def halo_source(cells, dz, dx):
    rows = cells
    if dz == -1:
        rows = cells[:4] if dx else cells[:3]
    elif dz == 1:
        rows = cells[4:] if dx else cells[5:]
    if dx == 0:
        return rows.astype(BF16)
    return pack_rows(rows[:, :8] if dx == -1 else rows[:, 8:]).astype(BF16)


def halo_target(padded, landed, dz, dx):
    if dx:
        half = landed.shape[0]
        landed = jnp.concatenate([landed[:, :8], landed[:, 8:]], axis=0)
        if dz == 1:
            landed = landed[1:]
        elif dz == -1:
            landed = landed[:3]
    rows = slice(3, 11) if dz == 0 else (slice(0, 3) if dz == 1 else slice(11, 14))
    columns = slice(8, 24) if dx == 0 else (slice(0, 8) if dx == 1 else slice(24, 32))
    padded[rows, columns, :] = landed


def halo_shape(dz, dx, chans):
    if dx == 0:
        return (3, 16, chans)
    return (4 if dz == 0 else 2, 16, chans)


def fused_kernel(
    sizes,
    scale,
    x_hbm,
    gout_hbm,
    dwk_hbm,
    dwb_hbm,
    gain_hbm,
    lnb_hbm,
    wexp_hbm,
    bexp_hbm,
    wred_hbm,
    bred_hbm,
    ls_hbm,
    out_ref,
    gin_ref,
    gexp_ref,
    gred_ref,
    gker_ref,
    gvec_ref,
    gbexp_ref,
    x_ref,
    gout_ref,
    dwk_ref,
    dwb_1d,
    gain_1d,
    lnb_1d,
    wexp,
    bexp_1d,
    wred,
    bred_1d,
    ls_1d,
    bexp_ref,
    pre_s,
    gact_s,
    xp,
    gp,
    work,
    xhat_s,
    lhs_t,
    act_s,
    gpre_s,
    main0,
    main1,
    rem,
    grad_out_blocks,
    landed0,
    xsend,
    xland,
    gsend,
    gland,
    small,
    small_send,
    small_land,
    zsend,
    zland,
    final,
    keeps,
    sends,
    lands,
    wsem,
    halo_sems,
    core_sems,
    part_sems,
    small_sems,
):
    zn, xn, rn = sizes
    z, x, r = lax.axis_index("rows"), lax.axis_index("cols"), lax.axis_index("rep")
    y, c = r // 2, r % 2
    chans = x_ref.shape[-1]
    hidden = wexp.shape[1]
    core_mate = {"rows": z, "cols": x, "rep": 2 * y + 1 - c}
    y_mate = {"rows": z, "cols": x, "rep": 2 * (1 - y) + c}
    x_mate = {"rows": z, "cols": 1 - x, "rep": r}

    def z_mate(d):
        return {"rows": (z + d) % zn, "cols": x, "rep": r}

    fetches = [
        pltpu.make_async_copy(source, target, wsem.at[n])
        for n, (source, target) in enumerate(
            (
                (x_hbm, x_ref),
                (gout_hbm, gout_ref),
                (ls_hbm, ls_1d),
                (wred_hbm, wred),
                (dwb_hbm, dwb_1d),
                (dwk_hbm, dwk_ref),
                (gain_hbm, gain_1d),
                (lnb_hbm, lnb_1d),
                (bexp_hbm, bexp_1d),
                (bred_hbm, bred_1d),
                (wexp_hbm, wexp),
            )
        )
    ]
    for copy in fetches:
        copy.start()

    def inside(a, b):
        return (a >= 0) & (a < zn) & (b >= 0) & (b < xn)

    barrier = pltpu.get_barrier_semaphore()
    greeted = jnp.int32(6)
    for mate in [core_mate, y_mate, x_mate] + [z_mate(d) for d in (1, 2, 3)]:
        pl.semaphore_signal(barrier, inc=1, device_id=mate, device_id_type=MESH)
    for dz, dx in DIRECTIONS:
        if dx == 0 or dz == 0:
            continue
        near = inside(z + dz, x + dx)

        @pl.when(near)
        def _():
            pl.semaphore_signal(
                barrier,
                inc=1,
                device_id={"rows": z + dz, "cols": x + dx, "rep": r},
                device_id_type=MESH,
            )

        greeted = greeted + near.astype(jnp.int32)

    xp[...] = jnp.zeros_like(xp)
    gp[...] = jnp.zeros_like(gp)
    small[...] = jnp.zeros_like(small)
    fetches[0].wait()
    cells = x_ref[0].astype(F32)
    for n, (dz, dx) in enumerate(DIRECTIONS):
        xsend[n][...] = halo_source(cells, dz, dx)
    xp[3:11, 8:24, :] = cells
    pl.semaphore_wait(barrier, greeted)

    def halo_copy(which, n):
        source, target = ((xsend, xland), (gsend, gland))[which]
        dz, dx = DIRECTIONS[n]
        return pltpu.make_async_remote_copy(
            src_ref=source[n],
            dst_ref=target[n],
            send_sem=halo_sems.at[which, 0, n],
            recv_sem=halo_sems.at[which, 1, n],
            device_id={"rows": z + dz, "cols": x + dx, "rep": r},
            device_id_type=MESH,
        )

    def halo_start(which):
        for n, (dz, dx) in enumerate(DIRECTIONS):
            pl.when(inside(z + dz, x + dx))(lambda n=n: halo_copy(which, n).start())

    def halo_finish(which, padded):
        landed = (xland, gland)[which]
        for n, (dz, dx) in enumerate(DIRECTIONS):

            @pl.when(inside(z - dz, x - dx))
            def _(n=n, dz=dz, dx=dx):
                halo_copy(which, n).wait_recv()
                halo_target(padded, landed[n][...].astype(F32), dz, dx)

    def halo_sent(which):
        for n, (dz, dx) in enumerate(DIRECTIONS):
            pl.when(inside(z + dz, x + dx))(lambda n=n: halo_copy(which, n).wait_send())

    halo_start(0)
    for copy in fetches[1:10]:
        copy.wait()

    def row(ref):
        return ref[...].reshape(1, -1)

    layer_scale, gain = row(ls_1d), row(gain_1d)
    bexp_ref[...] = row(bexp_1d)
    grad = gout_ref[0].astype(F32).reshape(-1, chans)
    scaled = grad * layer_scale
    g_branch = scaled.astype(BF16)
    small[52:53, :] = jnp.sum(scaled, axis=0, keepdims=True)
    contract_last = (((1,), (1,)), ((), ()))
    gact_s[...] = lax.dot_general(g_branch, wred[...], contract_last, preferred_element_type=F32)
    lhs_t[1] = scaled.T.astype(BF16).reshape(rn, chans // rn, 128)
    bias = row(dwb_1d)
    work[...] = jnp.broadcast_to(bias, work.shape)
    halo_finish(0, xp)

    def conv_chunk(n, carry):
        ch = pl.ds(pl.multiple_of(n * LANES, LANES), LANES)
        total = work[:, ch].reshape(8, 16, LANES)
        for j in range(7):
            shifted = xp[:, 5 + j : 21 + j, ch]
            for i in range(7):
                total = total + dwk_ref[i, j : j + 1, ch] * shifted[i : i + 8]
        work[:, ch] = total.reshape(128, LANES)
        return carry

    lax.fori_loop(0, chans // LANES, conv_chunk, 0)
    conv = work[...]
    centered = conv - jnp.mean(conv, axis=-1, keepdims=True)
    rstd = lax.rsqrt(jnp.mean(centered * centered, axis=-1, keepdims=True) + EPS)
    xhat = centered * rstd
    xhat_s[...] = xhat
    normed32 = xhat * gain + row(lnb_1d)
    normed = normed32.astype(BF16)
    lhs_t[0] = normed32.T.astype(BF16).reshape(rn, chans // rn, 128)
    fetches[10].wait()
    lefts_of = {}
    for owner, name in ((1 - c, "mate"), (c, "own")):
        left0 = jnp.concatenate([lhs_t[0, owner], lhs_t[0, 2 + owner]], axis=0)
        left1 = jnp.concatenate([lhs_t[1, owner], lhs_t[1, 2 + owner]], axis=0)
        lefts_of[name] = (left0, left1, jnp.concatenate([left0, left1], axis=1))

    def expand_group(n):
        at = slice(n * 3 * LANES, (n + 1) * 3 * LANES)
        pre_s[:, at] = jnp.dot(normed, wexp[:, at], preferred_element_type=F32)

    lower = lax.broadcasted_iota(jnp.int32, (64, LANES), 1) < LANES // 2
    zero = jnp.zeros((64, LANES), F32)

    def hidden_pair(n):
        here = n * 3 * LANES
        even = slice(2 * n * LANES, (2 * n + 1) * LANES)
        odd = slice((2 * n + 1) * LANES, (2 * n + 2) * LANES)
        sums = []
        for group in range(3):
            ch = slice(here + group * LANES, here + (group + 1) * LANES)
            sums.append(jnp.zeros((1, LANES), F32))
            for top in (0, 64):
                rows = slice(top, top + 64)
                after = slice(128 + top, 192 + top)
                pre = pre_s[rows, ch] + bexp_ref[:, ch]
                cdf = 0.5 * (1.0 + lax.erf(pre * INV_ROOT_TWO))
                act = pre * cdf
                pdf = jnp.exp(-0.5 * pre * pre) * INV_ROOT_TWO_PI
                g_pre = gact_s[rows, ch] * (cdf + pre * pdf)
                sums[-1] = sums[-1] + jnp.sum(g_pre, axis=0, keepdims=True)
                act_s[rows, ch] = act.astype(BF16)
                gpre_s[rows, ch] = g_pre.astype(BF16)
                if group == 1:
                    rolled = pltpu.roll(act, LANES // 2, 1)
                    rem[rows, even] = jnp.where(lower, g_pre, zero).astype(BF16)
                    rem[after, even] = jnp.where(lower, zero, rolled).astype(BF16)
                    rem[rows, odd] = jnp.where(lower, zero, g_pre).astype(BF16)
                    rem[after, odd] = jnp.where(lower, rolled, zero).astype(BF16)
                else:
                    to = odd if group else even
                    main0[rows, to] = g_pre.astype(BF16)
                    main1[rows, to] = act.astype(BF16)
        small[54 + n : 55 + n, :] = jnp.concatenate(sums, axis=1)

    def products(owner, lefts, zz):
        for k, right in enumerate((main0, main1, rem)):
            block = jnp.dot(
                lefts[k], right[:, 2 * zz * LANES : (2 * zz + 2) * LANES], preferred_element_type=F32
            ).astype(BF16)
            for xx in range(xn):
                for yy in range(2):
                    for h in range(2):
                        at = (2 * yy + h) * PIECE
                        grad_out_blocks[owner, 2 * k + h, yy, xx, zz] = block[
                            at : at + PIECE, xx * LANES : (xx + 1) * LANES
                        ]

    def core_copy(zz):
        return pltpu.make_async_remote_copy(
            src_ref=grad_out_blocks.at[1 - c, :, :, :, zz],
            dst_ref=landed0.at[:, :, :, zz],
            send_sem=core_sems.at[0, zz],
            recv_sem=core_sems.at[1, zz],
            device_id=core_mate,
            device_id_type=MESH,
        )

    parts = len(ORDERS)
    expand_group(0)
    expand_group(1)
    hidden_pair(0)
    for n in range(zn):
        products(1 - c, lefts_of["mate"], n)
        products(c, lefts_of["own"], n)
        if n + 2 < zn:
            expand_group(n + 2)
        if n + 1 < zn:
            hidden_pair(n + 1)
        core_copy(n).start()

    def place(dims, axis, index):
        return tuple(index if d == axis else slice(None) for d in dims)

    def stage_copies(p, s):
        axis = ORDERS[p][s]
        if axis == "z":
            return [
                pltpu.make_async_remote_copy(
                    src_ref=sends[p][s].at[d - 1],
                    dst_ref=lands[p][s].at[d - 1],
                    send_sem=part_sems.at[p, s, 0, d - 1],
                    recv_sem=part_sems.at[p, s, 1, d - 1],
                    device_id=z_mate(d),
                    device_id_type=MESH,
                )
                for d in (1, 2, 3)
            ]
        return [
            pltpu.make_async_remote_copy(
                src_ref=sends[p][s].at[0],
                dst_ref=lands[p][s].at[0],
                send_sem=part_sems.at[p, s, 0, 0],
                recv_sem=part_sems.at[p, s, 1, 0],
                device_id=y_mate if axis == "y" else x_mate,
                device_id_type=MESH,
            )
        ]

    def load(p, s, at):
        if s == 0:
            return grad_out_blocks[(c, p) + at].astype(F32) + landed0[(p,) + at].astype(F32)
        total = keeps[p][s - 1][at]
        for d in range(lands[p][s - 1].shape[0]):
            total = total + lands[p][s - 1][(d,) + at].astype(F32)
        return total

    def stage(p, s):
        if s:
            for copy in stage_copies(p, s - 1):
                copy.wait_recv()
        dims = [d for d in "yxz" if d not in ORDERS[p][:s]]
        if s == 3:
            final[p // 2, (p % 2) * PIECE : (p % 2 + 1) * PIECE, :] = load(p, s, ())
            return
        axis = ORDERS[p][s]
        copies = stage_copies(p, s)
        if axis == "z":
            for d in (1, 2, 3):
                sends[p][s][d - 1] = load(p, s, place(dims, "z", (z + d) % zn)).astype(BF16)
                copies[d - 1].start()
            keeps[p][s][...] = load(p, s, place(dims, "z", z))
        else:
            mine = y if axis == "y" else x
            sends[p][s][0] = load(p, s, place(dims, axis, 1 - mine)).astype(BF16)
            copies[0].start()
            keeps[p][s][...] = load(p, s, place(dims, axis, mine))

    for n in range(zn):
        core_copy(n).wait_recv()
    for p in range(parts):
        stage(p, 0)

    g_normed = lax.dot_general(gpre_s[...], wexp[...], contract_last, preferred_element_type=F32)
    xhat = xhat_s[...]
    small[50:51, :] = jnp.sum(g_normed * xhat, axis=0, keepdims=True)
    small[51:52, :] = jnp.sum(g_normed, axis=0, keepdims=True)
    gx = g_normed * gain
    g_conv = rstd * (
        gx
        - jnp.mean(gx, axis=-1, keepdims=True)
        - xhat * jnp.mean(gx * xhat, axis=-1, keepdims=True)
    )
    small[49:50, :] = jnp.sum(g_conv, axis=0, keepdims=True)
    g_cells = g_conv.reshape(8, 16, chans)
    for n, (dz, dx) in enumerate(DIRECTIONS):
        gsend[n][...] = halo_source(g_cells, dz, dx)
    halo_start(1)
    gp[3:11, 8:24, :] = g_cells

    branch = jnp.dot(act_s[...], wred[...], preferred_element_type=F32) + row(bred_1d)
    small[53:54, :] = jnp.sum(grad * branch, axis=0, keepdims=True)
    inner = x_ref[0].astype(F32).reshape(-1, chans)
    out_ref[0] = (inner + layer_scale * branch).astype(BF16).reshape(8, 16, chans)

    for p in range(3):
        stage(p, 1)

    def kernel_chunk(n, carry):
        ch = pl.ds(pl.multiple_of(n * LANES, LANES), LANES)
        own = gp[3:11, 8:24, ch]
        for j in range(7):
            shifted = xp[:, 5 + j : 21 + j, ch]
            for i in range(7):
                terms = jnp.sum((own * shifted[i : i + 8]).reshape(16, 8, LANES), axis=0)
                small[7 * i + j : 7 * i + j + 1, ch] = jnp.sum(terms, axis=0, keepdims=True)
        return carry

    lax.fori_loop(0, chans // LANES, kernel_chunk, 0)

    half = small.shape[0] // 2

    def small_copy(n, source, target, mate):
        return pltpu.make_async_remote_copy(
            src_ref=source,
            dst_ref=target,
            send_sem=small_sems.at[0, n],
            recv_sem=small_sems.at[1, n],
            device_id=mate,
            device_id_type=MESH,
        )

    moves = [small_copy(n, small_send.at[n], small_land.at[n], m) for n, m in enumerate((core_mate, y_mate, x_mate))]
    z_moves = [small_copy(2 + d, zsend, zland.at[d - 1], z_mate(d)) for d in (1, 2, 3)]
    other_rows = pl.ds(pl.multiple_of((1 - c) * half, half), half)
    my_rows = pl.ds(pl.multiple_of(c * half, half), half)
    small_send[0] = small[other_rows, :]
    moves[0].start()

    for p in range(3, parts):
        stage(p, 1)

    moves[0].wait_recv()
    small_send[1] = small[my_rows, :] + small_land[0]
    moves[1].start()
    for p in range(3):
        stage(p, 2)
    moves[1].wait_recv()
    small_send[2] = small_send[1] + small_land[1]
    moves[2].start()
    for p in range(3, parts):
        stage(p, 2)
    moves[2].wait_recv()
    zsend[...] = (small_send[2] + small_land[2]).astype(BF16)
    for move in z_moves:
        move.start()

    halo_finish(1, gp)

    def input_chunk(n, carry):
        ch = pl.ds(pl.multiple_of(n * LANES, LANES), LANES)
        total = gout_ref[0, :, :, ch].astype(F32)
        for j in range(7):
            shifted = gp[:, 11 - j : 27 - j, ch]
            for i in range(7):
                total = total + dwk_ref[i, j : j + 1, ch] * shifted[6 - i : 14 - i]
        gin_ref[0, :, :, ch] = total.astype(BF16)
        return carry

    lax.fori_loop(0, chans // LANES, input_chunk, 0)

    for move in z_moves:
        move.wait_recv()
    quarter = [zsend[...].astype(F32)] + [zland[d].astype(F32) for d in range(3)]
    total = jnp.zeros_like(quarter[0])
    for at in range(zn):
        d = (z - at) % zn
        term = quarter[0]
        for k in (1, 2, 3):
            term = jnp.where(d == k, quarter[k], term)
        total = total + term
    small_send[3] = total * scale
    last = small_copy(6, small_send.at[3], small_land.at[3], core_mate)
    last.start()

    for p in range(parts):
        stage(p, 3)
    blocks = final[...] * scale
    wide = LANES + LANES // 2
    m0, m1, mixed = blocks[0], blocks[1], blocks[2]
    first, second = mixed[:, : LANES // 2], mixed[:, LANES // 2 :]

    @pl.when(x == 0)
    def _():
        gexp_ref[:, :LANES] = m0
        gexp_ref[:, LANES:wide] = first
        gred_ref[:, :LANES] = m1
        gred_ref[:, LANES:wide] = second

    @pl.when(x == 1)
    def _():
        gexp_ref[...] = jnp.concatenate([second, m0], axis=1)
        gred_ref[...] = jnp.concatenate([first, m1], axis=1)

    last.wait_recv()
    small[my_rows, :] = small_send[3]
    small[other_rows, :] = small_land[3]
    for i in range(7):
        gker_ref[i] = small[7 * i : 7 * i + 7, :]
    gvec_ref[...] = small[49:54, :]
    for n in range(hidden // chans):
        bexp_ref[:, n * chans : (n + 1) * chans] = small[54 + n : 55 + n, :]
    gbexp_ref[...] = bexp_ref[...].reshape(-1)

    halo_sent(0)
    halo_sent(1)
    for n in range(zn):
        core_copy(n).wait_send()
    for p in range(parts):
        for s in range(3):
            for copy in stage_copies(p, s):
                copy.wait_send()
    for move in moves + z_moves + [last]:
        move.wait_send()


def fused(mesh_sizes, *args):
    (
        feature_map,
        dw_kernel,
        dw_bias,
        layer_norm_gain,
        layer_norm_bias,
        w_expand,
        b_expand,
        w_reduce,
        b_reduce,
        layer_scale,
        cotangent,
    ) = args
    zn, xn, rn = mesh_sizes
    _, height, width, chans = feature_map.shape
    hidden = w_expand.shape[1]
    pixels = height * width * zn * xn * rn
    scale = float(pixels) ** -0.5
    vmem = pl.BlockSpec(memory_space=pltpu.VMEM)
    hbm = pl.BlockSpec(memory_space=pltpu.HBM)
    parts = len(ORDERS)
    block = (PIECE, LANES)
    keeps, sends, lands = [], [], []
    for order in ORDERS:
        keeps.append([])
        sends.append([])
        lands.append([])
        for s in range(3):
            left = tuple(SIZES[d] for d in "yxz" if d not in order[: s + 1])
            copies = 3 if order[s] == "z" else 1
            keeps[-1].append(pltpu.VMEM(left + block, F32))
            sends[-1].append(pltpu.VMEM((copies,) + left + block, BF16))
            lands[-1].append(pltpu.VMEM((copies,) + left + block, BF16))
    halos = [pltpu.VMEM(halo_shape(dz, dx, chans), BF16) for dz, dx in DIRECTIONS]
    scratch = dict(
        x_ref=pltpu.VMEM(feature_map.shape, BF16),
        gout_ref=pltpu.VMEM(cotangent.shape, BF16),
        dwk_ref=pltpu.VMEM(dw_kernel.shape, F32),
        dwb_1d=pltpu.VMEM((chans,), F32),
        gain_1d=pltpu.VMEM((chans,), F32),
        lnb_1d=pltpu.VMEM((chans,), F32),
        wexp=pltpu.VMEM(w_expand.shape, BF16),
        bexp_1d=pltpu.VMEM((hidden,), F32),
        wred=pltpu.VMEM(w_reduce.shape, BF16),
        bred_1d=pltpu.VMEM((chans,), F32),
        ls_1d=pltpu.VMEM((chans,), F32),
        bexp_ref=pltpu.VMEM((1, hidden), F32),
        pre_s=pltpu.VMEM((128, hidden), F32),
        gact_s=pltpu.VMEM((128, hidden), F32),
        xp=pltpu.VMEM((14, 32, chans), F32),
        gp=pltpu.VMEM((14, 32, chans), F32),
        work=pltpu.VMEM((128, chans), F32),
        xhat_s=pltpu.VMEM((128, chans), F32),
        lhs_t=pltpu.VMEM((2, rn, chans // rn, 128), BF16),
        act_s=pltpu.VMEM((128, hidden), BF16),
        gpre_s=pltpu.VMEM((128, hidden), BF16),
        main0=pltpu.VMEM((128, 2 * zn * LANES), BF16),
        main1=pltpu.VMEM((128, 2 * zn * LANES), BF16),
        rem=pltpu.VMEM((256, 2 * zn * LANES), BF16),
        grad_out_blocks=pltpu.VMEM((2, parts, 2, xn, zn) + block, BF16),
        landed0=pltpu.VMEM((parts, 2, xn, zn) + block, BF16),
        xsend=list(halos),
        xland=list(halos),
        gsend=list(halos),
        gland=list(halos),
        small=pltpu.VMEM((64, chans), F32),
        small_send=pltpu.VMEM((4, 32, chans), F32),
        small_land=pltpu.VMEM((4, 32, chans), F32),
        zsend=pltpu.VMEM((32, chans), BF16),
        zland=pltpu.VMEM((3, 32, chans), BF16),
        final=pltpu.VMEM((3, 2 * PIECE, LANES), F32),
        keeps=keeps,
        sends=sends,
        lands=lands,
        wsem=pltpu.SemaphoreType.DMA((11,)),
        halo_sems=pltpu.SemaphoreType.DMA((2, 2, 8)),
        core_sems=pltpu.SemaphoreType.DMA((2, zn)),
        part_sems=pltpu.SemaphoreType.DMA((parts, 3, 2, 3)),
        small_sems=pltpu.SemaphoreType.DMA((2, 7)),
    )
    rows, columns = chans // rn, hidden // (zn * xn)
    outs = pl.pallas_call(
        functools.partial(fused_kernel, mesh_sizes, scale),
        out_shape=[
            jax.ShapeDtypeStruct(feature_map.shape, BF16),
            jax.ShapeDtypeStruct(feature_map.shape, BF16),
            jax.ShapeDtypeStruct((rows, columns), F32),
            jax.ShapeDtypeStruct((rows, columns), F32),
            jax.ShapeDtypeStruct(dw_kernel.shape, F32),
            jax.ShapeDtypeStruct((5, chans), F32),
            jax.ShapeDtypeStruct((hidden,), F32),
        ],
        in_specs=[hbm] * 11,
        out_specs=[vmem] * 7,
        scratch_shapes=list(scratch.values()),
        compiler_params=pltpu.CompilerParams(
            collective_id=0, has_side_effects=True, vmem_limit_bytes=VMEM_BYTES
        ),
    )(
        feature_map,
        cotangent,
        dw_kernel,
        dw_bias,
        layer_norm_gain,
        layer_norm_bias,
        w_expand,
        b_expand,
        w_reduce,
        b_reduce,
        layer_scale,
    )
    shapes = [jax.ShapeDtypeStruct(o.shape, o.dtype) for o in outs]
    return tuple(
        pl.pallas_call(
            write_out,
            out_shape=shapes,
            in_specs=[hbm] * 7,
            out_specs=[hbm] * 7,
            scratch_shapes=[pltpu.VMEM(o.shape, o.dtype) for o in outs]
            + [pltpu.SemaphoreType.DMA((2, 7))],
            compiler_params=pltpu.CompilerParams(vmem_limit_bytes=VMEM_BYTES),
        )(*outs)
    )


def write_out(*refs):
    sems = refs[21]
    reads = [pltpu.make_async_copy(refs[n], refs[14 + n], sems.at[0, n]) for n in range(7)]
    writes = [pltpu.make_async_copy(refs[14 + n], refs[7 + n], sems.at[1, n]) for n in range(7)]
    for copy in reads:
        copy.start()
    for read, write in zip(reads, writes):
        read.wait()
        write.start()
    for copy in writes:
        copy.wait()


def fits(sizes):
    return sizes == (4, 2, 4)


def solution(mesh):
    in_specs = (
        P("rep", "rows", "cols", None),
        P(),
        P(),
        P(),
        P(),
        P(),
        P(),
        P(),
        P(),
        P(),
        P("rep", "rows", "cols", None),
    )
    out_specs = (
        P("rep", "rows", "cols", None),
        P("rep", "rows", "cols", None),
        P("rep", ("rows", "cols")),
        P("rep", ("rows", "cols")),
        P(),
        P(),
        P(),
    )
    sizes = tuple(mesh.shape[a] for a in ("rows", "cols", "rep"))
    body = functools.partial(fused, sizes) if fits(sizes) else per_device
    return jax.shard_map(
        body, mesh=mesh, in_specs=in_specs, out_specs=out_specs, check_vma=False
    )
```

```python
import functools

import jax
import jax.numpy as jnp
from jax import lax
from jax.experimental import pallas as pl
from jax.experimental.pallas import tpu as pltpu
from jax.sharding import PartitionSpec as P

MESH = pl.DeviceIdType.MESH
F32, BF16 = jnp.float32, jnp.bfloat16
LANES = 128
PIECE = 48
VMEM_BYTES = 64 * 1024 * 1024
ORDERS = ("yxz", "xyz", "zyx", "xyz", "yxz", "xyz")
DIRECTIONS = ((-1, 0), (1, 0), (0, -1), (0, 1), (-1, -1), (-1, 1), (1, -1), (1, 1))
SIZES = {"y": 2, "x": 2, "z": 4}

EPS = 1e-06
INV_ROOT_TWO = 0.7071067811865476
INV_ROOT_TWO_PI = 0.3989422804014327


def extended(cells, sides, width):
    for axis, dim in sides:
        count = lax.axis_size(axis)
        ends = count - 1
        head = lax.slice_in_dim(cells, 0, width, axis=dim)
        tail = lax.slice_in_dim(cells, cells.shape[dim] - width, cells.shape[dim], axis=dim)
        cells = jnp.concatenate(
            [
                lax.ppermute(tail, axis, [(i, (i + 1) % count) for i in range(ends)]),
                cells,
                lax.ppermute(head, axis, [((i + 1) % count, i) for i in range(ends)]),
            ],
            axis=dim,
        )
    return cells


def depthwise(padded, kernel, height, width):
    total = jnp.zeros((height, width, padded.shape[-1]), jnp.float32)
    for i in range(7):
        for j in range(7):
            total = total + kernel[i, j] * padded[i : i + height, j : j + width].astype(jnp.float32)
    return total


def front_pass(
    xpad,
    gout,
    dw_kernel,
    dw_bias,
    layer_norm_gain,
    layer_norm_bias,
    w_expand,
    b_expand,
    w_reduce,
    b_reduce,
    layer_scale,
    height,
    width,
):
    chans = xpad.shape[-1]
    conv = depthwise(xpad, dw_kernel, height, width) + dw_bias
    flat = conv.reshape(-1, chans)
    centered_input = flat - jnp.mean(flat, axis=-1, keepdims=True)
    inverse_deviation = lax.rsqrt(
        jnp.mean(centered_input * centered_input, axis=-1, keepdims=True) + EPS
    )
    standardized_input = centered_input * inverse_deviation
    normalized_rows = (standardized_input * layer_norm_gain + layer_norm_bias).astype(jnp.bfloat16)
    pre = jnp.dot(normalized_rows, w_expand, preferred_element_type=jnp.float32) + b_expand
    cdf = 0.5 * (1.0 + lax.erf(pre * INV_ROOT_TWO))
    act = (pre * cdf).astype(jnp.bfloat16)
    branch = jnp.dot(act, w_reduce, preferred_element_type=jnp.float32) + b_reduce
    inner = xpad[3 : 3 + height, 3 : 3 + width].reshape(-1, chans).astype(jnp.float32)
    block_out = (inner + layer_scale * branch).astype(jnp.bfloat16).reshape(height, width, chans)
    grad = gout.reshape(-1, chans).astype(jnp.float32)
    scaled = grad * layer_scale
    g_branch = scaled.astype(jnp.bfloat16)
    g_scale = jnp.sum(grad * branch, axis=0)
    g_breduce = jnp.sum(scaled, axis=0)
    grad_reduce_t = lax.dot_general(
        g_branch, act, (((0,), (0,)), ((), ())), preferred_element_type=jnp.float32
    )
    g_act = lax.dot_general(
        g_branch, w_reduce, (((1,), (1,)), ((), ())), preferred_element_type=jnp.float32
    )
    pdf = jnp.exp(-0.5 * pre * pre) * INV_ROOT_TWO_PI
    g_pre = g_act * (cdf + pre * pdf)
    g_bexp = jnp.sum(g_pre, axis=0)
    g_pre_b = g_pre.astype(jnp.bfloat16)
    grad_expand = lax.dot_general(
        normalized_rows, g_pre_b, (((0,), (0,)), ((), ())), preferred_element_type=jnp.float32
    )
    grad_normalized = lax.dot_general(
        g_pre_b, w_expand, (((1,), (1,)), ((), ())), preferred_element_type=jnp.float32
    )
    grad_norm_gain = jnp.sum(grad_normalized * standardized_input, axis=0)
    g_lnbias = jnp.sum(grad_normalized, axis=0)
    scaled_grad_input = grad_normalized * layer_norm_gain
    grad_convolution = inverse_deviation * (
        scaled_grad_input
        - jnp.mean(scaled_grad_input, axis=-1, keepdims=True)
        - standardized_input
        * jnp.mean(scaled_grad_input * standardized_input, axis=-1, keepdims=True)
    )
    g_dwbias = jnp.sum(grad_convolution, axis=0)
    vectors = jnp.stack([g_dwbias, grad_norm_gain, g_lnbias, g_breduce, g_scale])
    return (
        block_out,
        grad_convolution.reshape(height, width, chans),
        grad_expand,
        grad_reduce_t,
        vectors,
        g_bexp,
    )


def back_pass(gpad, xpad, gout, dw_kernel, height, width):
    inner = gpad[3 : 3 + height, 3 : 3 + width]
    grad_in = gout.astype(jnp.float32)
    kernel_rows = []
    for i in range(7):
        row_terms = []
        for j in range(7):
            part = xpad[i : i + height, j : j + width].astype(jnp.float32)
            row_terms.append(jnp.sum(inner * part, axis=(0, 1)))
            grad_in = (
                grad_in + dw_kernel[i, j] * gpad[6 - i : 6 - i + height, 6 - j : 6 - j + width]
            )
        kernel_rows.append(jnp.stack(row_terms))
    return (grad_in.astype(jnp.bfloat16), jnp.stack(kernel_rows))


def per_device(
    feature_map,
    dw_kernel,
    dw_bias,
    layer_norm_gain,
    layer_norm_bias,
    w_expand,
    b_expand,
    w_reduce,
    b_reduce,
    layer_scale,
    cotangent,
):
    height, width = (feature_map.shape[1], feature_map.shape[2])
    xpad = extended(feature_map, (("rows", 1), ("cols", 2)), 3)[0]
    gout = cotangent[0]
    block_out, grad_convolution, gexp, gred, vectors, gbexp = front_pass(
        xpad,
        gout,
        dw_kernel,
        dw_bias,
        layer_norm_gain,
        layer_norm_bias,
        w_expand,
        b_expand,
        w_reduce,
        b_reduce,
        layer_scale,
        height,
        width,
    )
    stacked = jnp.stack([gexp, gred])
    gpad = extended(grad_convolution, (("rows", 0), ("cols", 1)), 3)
    grad_in, gker = back_pass(gpad, xpad, gout, dw_kernel, height, width)
    partial_sum = lax.psum_scatter(stacked, "rep", scatter_dimension=1, tiled=True)
    summed = lax.psum_scatter(partial_sum, ("rows", "cols"), scatter_dimension=2, tiled=True)
    gker, vectors, gbexp = lax.psum((gker, vectors, gbexp), ("rows", "cols", "rep"))
    count = lax.axis_size("rows") * height * lax.axis_size("cols") * width * lax.axis_size("rep")
    scale = 1.0 / jnp.sqrt(jnp.float32(count))
    return (
        block_out[None],
        grad_in[None],
        summed[0] * scale,
        summed[1] * scale,
        gker * scale,
        vectors * scale,
        gbexp * scale,
    )


def pack_rows(value):
    half = value.shape[0] // 2
    return jnp.concatenate([value[:half, :8], value[half:, :8]], axis=1)


def halo_source(cells, dz, dx):
    rows = cells
    if dz == -1:
        rows = cells[:4] if dx else cells[:3]
    elif dz == 1:
        rows = cells[4:] if dx else cells[5:]
    if dx == 0:
        return rows.astype(BF16)
    return pack_rows(rows[:, :8] if dx == -1 else rows[:, 8:]).astype(BF16)


def halo_target(padded, landed, dz, dx):
    if dx:
        half = landed.shape[0]
        landed = jnp.concatenate([landed[:, :8], landed[:, 8:]], axis=0)
        if dz == 1:
            landed = landed[1:]
        elif dz == -1:
            landed = landed[:3]
    rows = slice(3, 11) if dz == 0 else (slice(0, 3) if dz == 1 else slice(11, 14))
    columns = slice(8, 24) if dx == 0 else (slice(0, 8) if dx == 1 else slice(24, 32))
    padded[rows, columns, :] = landed


def halo_shape(dz, dx, chans):
    if dx == 0:
        return (3, 16, chans)
    return (4 if dz == 0 else 2, 16, chans)


def fused_kernel(
    sizes,
    scale,
    x_hbm,
    gout_hbm,
    dwk_hbm,
    dwb_hbm,
    gain_hbm,
    lnb_hbm,
    wexp_hbm,
    bexp_hbm,
    wred_hbm,
    bred_hbm,
    ls_hbm,
    out_ref,
    gin_ref,
    gexp_ref,
    gred_ref,
    gker_ref,
    gvec_ref,
    gbexp_ref,
    x_ref,
    gout_ref,
    dwk_ref,
    dwb_1d,
    gain_1d,
    lnb_1d,
    wexp,
    bexp_1d,
    wred,
    bred_1d,
    ls_1d,
    bexp_ref,
    pre_s,
    gact_s,
    xp,
    gp,
    work,
    xhat_s,
    lhs_t,
    act_s,
    gpre_s,
    main0,
    main1,
    rem,
    grad_out_blocks,
    landed0,
    xsend,
    xland,
    gsend,
    gland,
    small,
    small_send,
    small_land,
    zsend,
    zland,
    final,
    keeps,
    sends,
    lands,
    wsem,
    halo_sems,
    core_sems,
    part_sems,
    small_sems,
):
    zn, xn, rn = sizes
    z, x, r = lax.axis_index("rows"), lax.axis_index("cols"), lax.axis_index("rep")
    y, c = r // 2, r % 2
    chans = x_ref.shape[-1]
    hidden = wexp.shape[1]
    core_mate = {"rows": z, "cols": x, "rep": 2 * y + 1 - c}
    y_mate = {"rows": z, "cols": x, "rep": 2 * (1 - y) + c}
    x_mate = {"rows": z, "cols": 1 - x, "rep": r}

    def z_mate(d):
        return {"rows": (z + d) % zn, "cols": x, "rep": r}

    fetches = [
        pltpu.make_async_copy(source, target, wsem.at[n])
        for n, (source, target) in enumerate(
            (
                (x_hbm, x_ref),
                (gout_hbm, gout_ref),
                (ls_hbm, ls_1d),
                (wred_hbm, wred),
                (dwb_hbm, dwb_1d),
                (dwk_hbm, dwk_ref),
                (gain_hbm, gain_1d),
                (lnb_hbm, lnb_1d),
                (bexp_hbm, bexp_1d),
                (bred_hbm, bred_1d),
                (wexp_hbm, wexp),
            )
        )
    ]
    for copy in fetches:
        copy.start()

    def inside(a, b):
        return (a >= 0) & (a < zn) & (b >= 0) & (b < xn)

    barrier = pltpu.get_barrier_semaphore()
    greeted = jnp.int32(6)
    for mate in [core_mate, y_mate, x_mate] + [z_mate(d) for d in (1, 2, 3)]:
        pl.semaphore_signal(barrier, inc=1, device_id=mate, device_id_type=MESH)
    for dz, dx in DIRECTIONS:
        if dx == 0 or dz == 0:
            continue
        near = inside(z + dz, x + dx)

        @pl.when(near)
        def _():
            pl.semaphore_signal(
                barrier,
                inc=1,
                device_id={"rows": z + dz, "cols": x + dx, "rep": r},
                device_id_type=MESH,
            )

        greeted = greeted + near.astype(jnp.int32)

    xp[...] = jnp.zeros_like(xp)
    gp[...] = jnp.zeros_like(gp)
    small[...] = jnp.zeros_like(small)
    fetches[0].wait()
    cells = x_ref[0].astype(F32)
    for n, (dz, dx) in enumerate(DIRECTIONS):
        xsend[n][...] = halo_source(cells, dz, dx)
    xp[3:11, 8:24, :] = cells
    pl.semaphore_wait(barrier, greeted)

    def halo_copy(which, n):
        source, target = ((xsend, xland), (gsend, gland))[which]
        dz, dx = DIRECTIONS[n]
        return pltpu.make_async_remote_copy(
            src_ref=source[n],
            dst_ref=target[n],
            send_sem=halo_sems.at[which, 0, n],
            recv_sem=halo_sems.at[which, 1, n],
            device_id={"rows": z + dz, "cols": x + dx, "rep": r},
            device_id_type=MESH,
        )

    def halo_start(which):
        for n, (dz, dx) in enumerate(DIRECTIONS):
            pl.when(inside(z + dz, x + dx))(lambda n=n: halo_copy(which, n).start())

    def halo_finish(which, padded):
        landed = (xland, gland)[which]
        for n, (dz, dx) in enumerate(DIRECTIONS):

            @pl.when(inside(z - dz, x - dx))
            def _(n=n, dz=dz, dx=dx):
                halo_copy(which, n).wait_recv()
                halo_target(padded, landed[n][...].astype(F32), dz, dx)

    def halo_sent(which):
        for n, (dz, dx) in enumerate(DIRECTIONS):
            pl.when(inside(z + dz, x + dx))(lambda n=n: halo_copy(which, n).wait_send())

    halo_start(0)
    for copy in fetches[1:10]:
        copy.wait()

    def row(ref):
        return ref[...].reshape(1, -1)

    layer_scale, gain = row(ls_1d), row(gain_1d)
    bexp_ref[...] = row(bexp_1d)
    grad = gout_ref[0].astype(F32).reshape(-1, chans)
    scaled = grad * layer_scale
    g_branch = scaled.astype(BF16)
    small[52:53, :] = jnp.sum(scaled, axis=0, keepdims=True)
    contract_last = (((1,), (1,)), ((), ()))
    gact_s[...] = lax.dot_general(g_branch, wred[...], contract_last, preferred_element_type=F32)
    lhs_t[1] = scaled.T.astype(BF16).reshape(rn, chans // rn, 128)
    bias = row(dwb_1d)
    work[...] = jnp.broadcast_to(bias, work.shape)
    halo_finish(0, xp)

    def conv_chunk(n, carry):
        ch = pl.ds(pl.multiple_of(n * LANES, LANES), LANES)
        total = work[:, ch].reshape(8, 16, LANES)
        for j in range(7):
            shifted = xp[:, 5 + j : 21 + j, ch]
            for i in range(7):
                total = total + dwk_ref[i, j : j + 1, ch] * shifted[i : i + 8]
        work[:, ch] = total.reshape(128, LANES)
        return carry

    lax.fori_loop(0, chans // LANES, conv_chunk, 0)
    conv = work[...]
    centered = conv - jnp.mean(conv, axis=-1, keepdims=True)
    rstd = lax.rsqrt(jnp.mean(centered * centered, axis=-1, keepdims=True) + EPS)
    xhat = centered * rstd
    xhat_s[...] = xhat
    normed32 = xhat * gain + row(lnb_1d)
    normed = normed32.astype(BF16)
    lhs_t[0] = normed32.T.astype(BF16).reshape(rn, chans // rn, 128)
    fetches[10].wait()
    lefts_of = {}
    for owner, name in ((1 - c, "mate"), (c, "own")):
        left0 = jnp.concatenate([lhs_t[0, owner], lhs_t[0, 2 + owner]], axis=0)
        left1 = jnp.concatenate([lhs_t[1, owner], lhs_t[1, 2 + owner]], axis=0)
        lefts_of[name] = (left0, left1, jnp.concatenate([left0, left1], axis=1))

    def expand_group(n):
        at = slice(n * 3 * LANES, (n + 1) * 3 * LANES)
        pre_s[:, at] = jnp.dot(normed, wexp[:, at], preferred_element_type=F32)

    lower = lax.broadcasted_iota(jnp.int32, (64, LANES), 1) < LANES // 2
    zero = jnp.zeros((64, LANES), F32)

    def hidden_pair(n):
        here = n * 3 * LANES
        even = slice(2 * n * LANES, (2 * n + 1) * LANES)
        odd = slice((2 * n + 1) * LANES, (2 * n + 2) * LANES)
        sums = []
        for group in range(3):
            ch = slice(here + group * LANES, here + (group + 1) * LANES)
            sums.append(jnp.zeros((1, LANES), F32))
            for top in (0, 64):
                rows = slice(top, top + 64)
                after = slice(128 + top, 192 + top)
                pre = pre_s[rows, ch] + bexp_ref[:, ch]
                cdf = 0.5 * (1.0 + lax.erf(pre * INV_ROOT_TWO))
                act = pre * cdf
                pdf = jnp.exp(-0.5 * pre * pre) * INV_ROOT_TWO_PI
                g_pre = gact_s[rows, ch] * (cdf + pre * pdf)
                sums[-1] = sums[-1] + jnp.sum(g_pre, axis=0, keepdims=True)
                act_s[rows, ch] = act.astype(BF16)
                gpre_s[rows, ch] = g_pre.astype(BF16)
                if group == 1:
                    rolled = pltpu.roll(act, LANES // 2, 1)
                    rem[rows, even] = jnp.where(lower, g_pre, zero).astype(BF16)
                    rem[after, even] = jnp.where(lower, zero, rolled).astype(BF16)
                    rem[rows, odd] = jnp.where(lower, zero, g_pre).astype(BF16)
                    rem[after, odd] = jnp.where(lower, rolled, zero).astype(BF16)
                else:
                    to = odd if group else even
                    main0[rows, to] = g_pre.astype(BF16)
                    main1[rows, to] = act.astype(BF16)
        small[54 + n : 55 + n, :] = jnp.concatenate(sums, axis=1)

    def products(owner, lefts, zz):
        for k, right in enumerate((main0, main1, rem)):
            block = jnp.dot(
                lefts[k], right[:, 2 * zz * LANES : (2 * zz + 2) * LANES], preferred_element_type=F32
            ).astype(BF16)
            for xx in range(xn):
                for yy in range(2):
                    for h in range(2):
                        at = (2 * yy + h) * PIECE
                        grad_out_blocks[owner, 2 * k + h, yy, xx, zz] = block[
                            at : at + PIECE, xx * LANES : (xx + 1) * LANES
                        ]

    def core_copy(zz):
        return pltpu.make_async_remote_copy(
            src_ref=grad_out_blocks.at[1 - c, :, :, :, zz],
            dst_ref=landed0.at[:, :, :, zz],
            send_sem=core_sems.at[0, zz],
            recv_sem=core_sems.at[1, zz],
            device_id=core_mate,
            device_id_type=MESH,
        )

    parts = len(ORDERS)
    expand_group(0)
    expand_group(1)
    hidden_pair(0)
    for n in range(zn):
        products(1 - c, lefts_of["mate"], n)
        products(c, lefts_of["own"], n)
        if n + 2 < zn:
            expand_group(n + 2)
        if n + 1 < zn:
            hidden_pair(n + 1)
        core_copy(n).start()

    def place(dims, axis, index):
        return tuple(index if d == axis else slice(None) for d in dims)

    def stage_copies(p, s):
        axis = ORDERS[p][s]
        if axis == "z":
            return [
                pltpu.make_async_remote_copy(
                    src_ref=sends[p][s].at[d - 1],
                    dst_ref=lands[p][s].at[d - 1],
                    send_sem=part_sems.at[p, s, 0, d - 1],
                    recv_sem=part_sems.at[p, s, 1, d - 1],
                    device_id=z_mate(d),
                    device_id_type=MESH,
                )
                for d in (1, 2, 3)
            ]
        return [
            pltpu.make_async_remote_copy(
                src_ref=sends[p][s].at[0],
                dst_ref=lands[p][s].at[0],
                send_sem=part_sems.at[p, s, 0, 0],
                recv_sem=part_sems.at[p, s, 1, 0],
                device_id=y_mate if axis == "y" else x_mate,
                device_id_type=MESH,
            )
        ]

    def load(p, s, at):
        if s == 0:
            return grad_out_blocks[(c, p) + at].astype(F32) + landed0[(p,) + at].astype(F32)
        total = keeps[p][s - 1][at]
        for d in range(lands[p][s - 1].shape[0]):
            total = total + lands[p][s - 1][(d,) + at].astype(F32)
        return total

    def stage(p, s):
        if s:
            for copy in stage_copies(p, s - 1):
                copy.wait_recv()
        dims = [d for d in "yxz" if d not in ORDERS[p][:s]]
        if s == 3:
            final[p // 2, (p % 2) * PIECE : (p % 2 + 1) * PIECE, :] = load(p, s, ())
            return
        axis = ORDERS[p][s]
        copies = stage_copies(p, s)
        if axis == "z":
            for d in (1, 2, 3):
                sends[p][s][d - 1] = load(p, s, place(dims, "z", (z + d) % zn)).astype(BF16)
                copies[d - 1].start()
            keeps[p][s][...] = load(p, s, place(dims, "z", z))
        else:
            mine = y if axis == "y" else x
            sends[p][s][0] = load(p, s, place(dims, axis, 1 - mine)).astype(BF16)
            copies[0].start()
            keeps[p][s][...] = load(p, s, place(dims, axis, mine))

    for n in range(zn):
        core_copy(n).wait_recv()
    for p in range(parts):
        stage(p, 0)

    g_normed = lax.dot_general(gpre_s[...], wexp[...], contract_last, preferred_element_type=F32)
    xhat = xhat_s[...]
    small[50:51, :] = jnp.sum(g_normed * xhat, axis=0, keepdims=True)
    small[51:52, :] = jnp.sum(g_normed, axis=0, keepdims=True)
    gx = g_normed * gain
    g_conv = rstd * (
        gx
        - jnp.mean(gx, axis=-1, keepdims=True)
        - xhat * jnp.mean(gx * xhat, axis=-1, keepdims=True)
    )
    small[49:50, :] = jnp.sum(g_conv, axis=0, keepdims=True)
    g_cells = g_conv.reshape(8, 16, chans)
    for n, (dz, dx) in enumerate(DIRECTIONS):
        gsend[n][...] = halo_source(g_cells, dz, dx)
    halo_start(1)
    gp[3:11, 8:24, :] = g_cells
    stage(0, 1)
    stage(1, 1)

    branch = jnp.dot(act_s[...], wred[...], preferred_element_type=F32) + row(bred_1d)
    small[53:54, :] = jnp.sum(grad * branch, axis=0, keepdims=True)
    inner = x_ref[0].astype(F32).reshape(-1, chans)
    out_ref[0] = (inner + layer_scale * branch).astype(BF16).reshape(8, 16, chans)

    stage(2, 1)

    def kernel_chunk(n, carry):
        ch = pl.ds(pl.multiple_of(n * LANES, LANES), LANES)
        own = gp[3:11, 8:24, ch]
        for j in range(7):
            shifted = xp[:, 5 + j : 21 + j, ch]
            for i in range(7):
                terms = jnp.sum((own * shifted[i : i + 8]).reshape(16, 8, LANES), axis=0)
                small[7 * i + j : 7 * i + j + 1, ch] = jnp.sum(terms, axis=0, keepdims=True)
        return carry

    lax.fori_loop(0, chans // LANES, kernel_chunk, 0)

    half = small.shape[0] // 2

    def small_copy(n, source, target, mate):
        return pltpu.make_async_remote_copy(
            src_ref=source,
            dst_ref=target,
            send_sem=small_sems.at[0, n],
            recv_sem=small_sems.at[1, n],
            device_id=mate,
            device_id_type=MESH,
        )

    moves = [small_copy(n, small_send.at[n], small_land.at[n], m) for n, m in enumerate((core_mate, y_mate, x_mate))]
    z_moves = [small_copy(2 + d, zsend, zland.at[d - 1], z_mate(d)) for d in (1, 2, 3)]
    other_rows = pl.ds(pl.multiple_of((1 - c) * half, half), half)
    my_rows = pl.ds(pl.multiple_of(c * half, half), half)
    small_send[0] = small[other_rows, :]
    moves[0].start()

    for p in range(3, parts):
        stage(p, 1)

    moves[0].wait_recv()
    small_send[1] = small[my_rows, :] + small_land[0]
    moves[1].start()
    for p in range(3):
        stage(p, 2)
    moves[1].wait_recv()
    small_send[2] = small_send[1] + small_land[1]
    moves[2].start()
    for p in range(3, parts):
        stage(p, 2)
    moves[2].wait_recv()
    zsend[...] = (small_send[2] + small_land[2]).astype(BF16)
    for move in z_moves:
        move.start()

    halo_finish(1, gp)

    def input_chunk(n, carry):
        ch = pl.ds(pl.multiple_of(n * LANES, LANES), LANES)
        total = gout_ref[0, :, :, ch].astype(F32)
        for j in range(7):
            shifted = gp[:, 11 - j : 27 - j, ch]
            for i in range(7):
                total = total + dwk_ref[i, j : j + 1, ch] * shifted[6 - i : 14 - i]
        gin_ref[0, :, :, ch] = total.astype(BF16)
        return carry

    lax.fori_loop(0, chans // LANES, input_chunk, 0)

    for move in z_moves:
        move.wait_recv()
    quarter = [zsend[...].astype(F32)] + [zland[d].astype(F32) for d in range(3)]
    total = jnp.zeros_like(quarter[0])
    for at in range(zn):
        d = (z - at) % zn
        term = quarter[0]
        for k in (1, 2, 3):
            term = jnp.where(d == k, quarter[k], term)
        total = total + term
    small_send[3] = total * scale
    last = small_copy(6, small_send.at[3], small_land.at[3], core_mate)
    last.start()

    for p in range(parts):
        stage(p, 3)
    blocks = final[...] * scale
    wide = LANES + LANES // 2
    m0, m1, mixed = blocks[0], blocks[1], blocks[2]
    first, second = mixed[:, : LANES // 2], mixed[:, LANES // 2 :]

    @pl.when(x == 0)
    def _():
        gexp_ref[:, :LANES] = m0
        gexp_ref[:, LANES:wide] = first
        gred_ref[:, :LANES] = m1
        gred_ref[:, LANES:wide] = second

    @pl.when(x == 1)
    def _():
        gexp_ref[...] = jnp.concatenate([second, m0], axis=1)
        gred_ref[...] = jnp.concatenate([first, m1], axis=1)

    last.wait_recv()
    small[my_rows, :] = small_send[3]
    small[other_rows, :] = small_land[3]
    for i in range(7):
        gker_ref[i] = small[7 * i : 7 * i + 7, :]
    gvec_ref[...] = small[49:54, :]
    for n in range(hidden // chans):
        bexp_ref[:, n * chans : (n + 1) * chans] = small[54 + n : 55 + n, :]
    gbexp_ref[...] = bexp_ref[...].reshape(-1)

    halo_sent(0)
    halo_sent(1)
    for n in range(zn):
        core_copy(n).wait_send()
    for p in range(parts):
        for s in range(3):
            for copy in stage_copies(p, s):
                copy.wait_send()
    for move in moves + z_moves + [last]:
        move.wait_send()


def fused(mesh_sizes, *args):
    (
        feature_map,
        dw_kernel,
        dw_bias,
        layer_norm_gain,
        layer_norm_bias,
        w_expand,
        b_expand,
        w_reduce,
        b_reduce,
        layer_scale,
        cotangent,
    ) = args
    zn, xn, rn = mesh_sizes
    _, height, width, chans = feature_map.shape
    hidden = w_expand.shape[1]
    pixels = height * width * zn * xn * rn
    scale = float(pixels) ** -0.5
    vmem = pl.BlockSpec(memory_space=pltpu.VMEM)
    hbm = pl.BlockSpec(memory_space=pltpu.HBM)
    parts = len(ORDERS)
    block = (PIECE, LANES)
    keeps, sends, lands = [], [], []
    for order in ORDERS:
        keeps.append([])
        sends.append([])
        lands.append([])
        for s in range(3):
            left = tuple(SIZES[d] for d in "yxz" if d not in order[: s + 1])
            copies = 3 if order[s] == "z" else 1
            keeps[-1].append(pltpu.VMEM(left + block, F32))
            sends[-1].append(pltpu.VMEM((copies,) + left + block, BF16))
            lands[-1].append(pltpu.VMEM((copies,) + left + block, BF16))
    halos = [pltpu.VMEM(halo_shape(dz, dx, chans), BF16) for dz, dx in DIRECTIONS]
    scratch = dict(
        x_ref=pltpu.VMEM(feature_map.shape, BF16),
        gout_ref=pltpu.VMEM(cotangent.shape, BF16),
        dwk_ref=pltpu.VMEM(dw_kernel.shape, F32),
        dwb_1d=pltpu.VMEM((chans,), F32),
        gain_1d=pltpu.VMEM((chans,), F32),
        lnb_1d=pltpu.VMEM((chans,), F32),
        wexp=pltpu.VMEM(w_expand.shape, BF16),
        bexp_1d=pltpu.VMEM((hidden,), F32),
        wred=pltpu.VMEM(w_reduce.shape, BF16),
        bred_1d=pltpu.VMEM((chans,), F32),
        ls_1d=pltpu.VMEM((chans,), F32),
        bexp_ref=pltpu.VMEM((1, hidden), F32),
        pre_s=pltpu.VMEM((128, hidden), F32),
        gact_s=pltpu.VMEM((128, hidden), F32),
        xp=pltpu.VMEM((14, 32, chans), F32),
        gp=pltpu.VMEM((14, 32, chans), F32),
        work=pltpu.VMEM((128, chans), F32),
        xhat_s=pltpu.VMEM((128, chans), F32),
        lhs_t=pltpu.VMEM((2, rn, chans // rn, 128), BF16),
        act_s=pltpu.VMEM((128, hidden), BF16),
        gpre_s=pltpu.VMEM((128, hidden), BF16),
        main0=pltpu.VMEM((128, 2 * zn * LANES), BF16),
        main1=pltpu.VMEM((128, 2 * zn * LANES), BF16),
        rem=pltpu.VMEM((256, 2 * zn * LANES), BF16),
        grad_out_blocks=pltpu.VMEM((2, parts, 2, xn, zn) + block, BF16),
        landed0=pltpu.VMEM((parts, 2, xn, zn) + block, BF16),
        xsend=list(halos),
        xland=list(halos),
        gsend=list(halos),
        gland=list(halos),
        small=pltpu.VMEM((64, chans), F32),
        small_send=pltpu.VMEM((4, 32, chans), F32),
        small_land=pltpu.VMEM((4, 32, chans), F32),
        zsend=pltpu.VMEM((32, chans), BF16),
        zland=pltpu.VMEM((3, 32, chans), BF16),
        final=pltpu.VMEM((3, 2 * PIECE, LANES), F32),
        keeps=keeps,
        sends=sends,
        lands=lands,
        wsem=pltpu.SemaphoreType.DMA((11,)),
        halo_sems=pltpu.SemaphoreType.DMA((2, 2, 8)),
        core_sems=pltpu.SemaphoreType.DMA((2, zn)),
        part_sems=pltpu.SemaphoreType.DMA((parts, 3, 2, 3)),
        small_sems=pltpu.SemaphoreType.DMA((2, 7)),
    )
    rows, columns = chans // rn, hidden // (zn * xn)
    outs = pl.pallas_call(
        functools.partial(fused_kernel, mesh_sizes, scale),
        out_shape=[
            jax.ShapeDtypeStruct(feature_map.shape, BF16),
            jax.ShapeDtypeStruct(feature_map.shape, BF16),
            jax.ShapeDtypeStruct((rows, columns), F32),
            jax.ShapeDtypeStruct((rows, columns), F32),
            jax.ShapeDtypeStruct(dw_kernel.shape, F32),
            jax.ShapeDtypeStruct((5, chans), F32),
            jax.ShapeDtypeStruct((hidden,), F32),
        ],
        in_specs=[hbm] * 11,
        out_specs=[vmem] * 7,
        scratch_shapes=list(scratch.values()),
        compiler_params=pltpu.CompilerParams(
            collective_id=0, has_side_effects=True, vmem_limit_bytes=VMEM_BYTES
        ),
    )(
        feature_map,
        cotangent,
        dw_kernel,
        dw_bias,
        layer_norm_gain,
        layer_norm_bias,
        w_expand,
        b_expand,
        w_reduce,
        b_reduce,
        layer_scale,
    )
    shapes = [jax.ShapeDtypeStruct(o.shape, o.dtype) for o in outs]
    return tuple(
        pl.pallas_call(
            write_out,
            out_shape=shapes,
            in_specs=[hbm] * 7,
            out_specs=[hbm] * 7,
            scratch_shapes=[pltpu.VMEM(o.shape, o.dtype) for o in outs]
            + [pltpu.SemaphoreType.DMA((2, 7))],
            compiler_params=pltpu.CompilerParams(vmem_limit_bytes=VMEM_BYTES),
        )(*outs)
    )


def write_out(*refs):
    sems = refs[21]
    reads = [pltpu.make_async_copy(refs[n], refs[14 + n], sems.at[0, n]) for n in range(7)]
    writes = [pltpu.make_async_copy(refs[14 + n], refs[7 + n], sems.at[1, n]) for n in range(7)]
    for copy in reads:
        copy.start()
    for read, write in zip(reads, writes):
        read.wait()
        write.start()
    for copy in writes:
        copy.wait()


def fits(sizes):
    return sizes == (4, 2, 4)


def solution(mesh):
    in_specs = (
        P("rep", "rows", "cols", None),
        P(),
        P(),
        P(),
        P(),
        P(),
        P(),
        P(),
        P(),
        P(),
        P("rep", "rows", "cols", None),
    )
    out_specs = (
        P("rep", "rows", "cols", None),
        P("rep", "rows", "cols", None),
        P("rep", ("rows", "cols")),
        P("rep", ("rows", "cols")),
        P(),
        P(),
        P(),
    )
    sizes = tuple(mesh.shape[a] for a in ("rows", "cols", "rep"))
    body = functools.partial(fused, sizes) if fits(sizes) else per_device
    return jax.shard_map(
        body, mesh=mesh, in_specs=in_specs, out_specs=out_specs, check_vma=False
    )
```
